256 devices in a mesh: row: 16 (over x, y_hi, core), col: 16 (over y_lo, z).
Axes of the slice: x: 4, y: 4 (y_hi: 2, y_lo: 2; y = y_hi * 2 + y_lo), z: 8, core: 2. Of those that a mesh axis runs over, the one named last changes fastest.
Arguments:
- pair: bfloat16 [2048, 64, 128], P('row', 'col'), may hold values from -6 to 6
- norm_gain: float32 [128], replicated, may hold values from 0.1 to 1.9
- norm_offset: float32 [128], replicated, may hold values from -3 to 3
- w_query: bfloat16 [128, 128], replicated, may hold values from -0.5 to 0.5
- w_key: bfloat16 [128, 128], replicated, may hold values from -0.5 to 0.5
- w_value: bfloat16 [128, 128], replicated, may hold values from -0.5 to 0.5
- w_gate: bfloat16 [128, 128], replicated, may hold values from -0.5 to 0.5
- gate_bias: float32 [128], replicated, may hold values from -4 to 4
- w_out: bfloat16 [128, 128], replicated, may hold values from -0.5 to 0.5
- out_bias: float32 [128], replicated, may hold values from -3 to 3
- bias: bfloat16 [4, 2048, 2048], P(None, 'row', 'col'), may hold values from -16 to 310
- chain_offset: float32 [4], replicated, may hold values from -3 to 1
- chain_ids: int32 [2048], replicated, may hold values from 0 to 7, never falling along the last dimension, each value on 1 to 512 neighbouring positions
- tile_mask: int32 [16, 16], replicated, may hold values from 0 to 1, as said below
Outputs:
- update: bfloat16 [2048, 64, 128], P('row', 'col')
The draws below stay inside these ranges and needn't reach their ends.
Inputs may be any that keep to these rules, and one draw needn't show every extreme that they name: `tile_mask`: every tile on the diagonal is 1; each block row holds at most 8 ones, and the last block row holds exactly that many.
All inputs are finite; a program needn't handle non-finite values.
Results may differ from the reference program's by a relative error of at most 0.0047.
Values may be sent and summed in bfloat16 or wider, within the bound.
A program may use at most 128 MiB of HBM per device.

```python
import math
import jax
import jax.numpy as jnp
import numpy as np
from jax import lax

C = 128
H = 4
DH = 32
TILE = 128
COL_DEV = 4
HD = 128
N = 2048
COLS = 64
NB = 16


def draw_bias(key, part):
    key = jax.random.fold_in(key, 11)
    first, second = jax.random.split(key, 2)
    row_scale = jnp.exp(jax.random.uniform(second, (H, N, 1), jnp.float32, math.log(0.3), math.log(3.0)))
    base = jnp.clip(jax.random.normal(first, (H, N, N), jnp.float32) * row_scale, -16.0, 16.0)
    return base.astype(jnp.bfloat16)


def draw_tile_mask(key, part):
    key = jax.random.fold_in(key, 23)
    blocks = N // TILE
    row_keys = jax.random.split(key, blocks)
    orders = jax.vmap(lambda single: jax.random.permutation(single, blocks))(row_keys)
    ranking = jnp.argsort(orders, axis=1).astype(jnp.int32)
    block_row = lax.broadcasted_iota(jnp.int32, (blocks, blocks), 0)
    block_col = lax.broadcasted_iota(jnp.int32, (blocks, blocks), 1)
    on_diag = block_row == block_col
    wanted = 1 + (blocks // 2 - 1) * block_row[:, :1] // max(blocks - 1, 1)
    diag_rank = jnp.sum(jnp.where(on_diag, ranking, 0), axis=1, keepdims=True)
    threshold = wanted - 1 + (diag_rank < wanted - 1).astype(jnp.int32)
    return jnp.where(on_diag | (ranking < threshold), 1, 0).astype(jnp.int32)


def levels(own_key, extent, shards, smallest, top_value):
    level, own = 1.0, jax.random.fold_in(own_key, 6)
    for dim, blocks in shards:
        heights = jnp.exp(jax.random.uniform(jax.random.fold_in(own, dim), (blocks,), jnp.float32, smallest / len(shards), top_value / len(shards)))
        level = level * jnp.repeat(heights, extent[dim] // blocks).reshape([-1 if axis == dim else 1 for axis in range(len(extent))])
    return level


def split_up(number_of, total, most, lean):
    weights = [(1 << 20) // math.isqrt(standing ** lean) + 1 for standing in range(2, number_of + 1)]
    surplus, counts = total - most - (number_of - 1), [1] * (number_of - 1)
    while surplus > 0:
        free = [i for i in range(number_of - 1) if counts[i] < most]
        mass, budget = sum([weights[i] for i in free]), surplus
        for i in free:
            addition = min(most - counts[i], max(1, budget * weights[i] // mass), surplus)
            counts[i] = counts[i] + addition
            surplus = surplus - addition
    return np.array([most] + counts)


def ragged(own_key, amount, total, reach, lean):
    if amount == 2:
        one = jax.random.randint(own_key, (), max(1, total - reach), min(reach, total - 1) + 1)
        return jnp.stack([one, total - one])
    lengths = jnp.asarray(split_up(amount, total, reach, lean), jnp.int32)
    pairs = (amount - 1) // 2
    giver, receiver = lengths[1:1 + 2 * pairs:2], lengths[2:2 + 2 * pairs:2]
    room = jnp.minimum(giver - 1, reach - receiver)
    shifted = jax.random.randint(jax.random.fold_in(own_key, 1), (pairs,), 0, 1 << 20) % (room + 1)
    lengths = lengths.at[1:1 + 2 * pairs:2].set(giver - shifted).at[2:2 + 2 * pairs:2].set(receiver + shifted)
    return lengths[jax.random.permutation(jax.random.fold_in(own_key, 2), amount)]


def bell_draw(own_key, extent, width, limit, pieces=(), held_as=jnp.bfloat16):
    drawn = jax.random.normal(own_key, extent, jnp.float32) * width
    if len(pieces) > 0:
        drawn = levels(own_key, extent, pieces, -0.22, 0.18) * drawn
    return jnp.clip(drawn, min=-limit, max=limit).astype(held_as)


def setup_inputs(seed: int = 0) -> dict:
    splits = jax.random.split(jax.random.key(seed), 15)
    pair = bell_draw(splits[0], (N, COLS, C), 1.0, 6.0, ((0, 16), (1, 16)))
    norm_gain = jnp.clip(1.0 + 0.18 * jax.random.normal(splits[1], (C,), jnp.float32), 0.1, 1.9)
    norm_offset = bell_draw(splits[2], (C,), 0.5, 3.0, (), jnp.float32)
    w_query = bell_draw(splits[3], (C, HD), C ** -0.5, 0.5)
    w_key = bell_draw(splits[4], (C, HD), C ** -0.5, 0.5)
    w_value = bell_draw(splits[5], (C, HD), C ** -0.5, 0.5)
    w_gate = bell_draw(splits[6], (C, HD), C ** -0.5, 0.5)
    gate_bias = bell_draw(splits[7], (HD,), 1.0, 4.0, (), jnp.float32)
    w_out = bell_draw(splits[8], (HD, C), HD ** -0.5, 0.5)
    out_bias = bell_draw(splits[9], (C,), 0.5, 3.0, (), jnp.float32)
    bias = draw_bias(jax.random.fold_in(splits[14], 71), 0)
    chain_offset = jnp.clip(jax.random.uniform(splits[11], (H,), jnp.float32, -3.0, 1.0), -3.0, 1.0)
    chain_ids = jnp.searchsorted(jnp.cumsum(ragged(splits[12], 8, N, N // 4, 1)), jnp.arange(N), side="right").astype(jnp.int32)
    tile_mask = draw_tile_mask(jax.random.fold_in(splits[14], 71), 0)
    return {"pair": pair, "norm_gain": norm_gain, "norm_offset": norm_offset, "w_query": w_query, "w_key": w_key, "w_value": w_value, "w_gate": w_gate, "gate_bias": gate_bias, "w_out": w_out, "out_bias": out_bias, "bias": bias, "chain_offset": chain_offset, "chain_ids": chain_ids, "tile_mask": tile_mask}


def layer_norm(pair, norm_gain, norm_offset):
    values = pair.astype(jnp.float32)
    center = values - lax.optimization_barrier(jnp.mean(values, -1, keepdims=True))
    spread = lax.optimization_barrier(jnp.mean(center * center, -1, keepdims=True))
    return (center * lax.rsqrt(spread + 1e-05) * norm_gain + norm_offset).astype(jnp.bfloat16)

def reference(pair, norm_gain, norm_offset, w_query, w_key, w_value, w_gate, gate_bias, w_out, out_bias, bias, chain_offset, chain_ids, tile_mask):
    normed = layer_norm(pair, norm_gain, norm_offset).reshape(N * COLS, C)
    scale = 1.0 / DH ** 0.5
    query = (jnp.dot(normed, w_query, preferred_element_type=jnp.float32) * scale).astype(jnp.bfloat16).reshape(N, COLS, H, DH)
    key = jnp.dot(normed, w_key, preferred_element_type=jnp.float32).astype(jnp.bfloat16).reshape(N, COLS, H, DH)
    value = jnp.dot(normed, w_value, preferred_element_type=jnp.float32).astype(jnp.bfloat16).reshape(N, COLS, H, DH)
    gate = jax.nn.sigmoid(jnp.dot(normed, w_gate, preferred_element_type=jnp.float32) + gate_bias)
    col_blocks = COLS // COL_DEV
    pairs_count = NB * col_blocks
    flat = jnp.arange(pairs_count, dtype=jnp.int32)

    def attend_block(which):
        qblock = (which // col_blocks).astype(jnp.int32)
        cblock = (which % col_blocks).astype(jnp.int32)
        zero = jnp.int32(0)
        queries = lax.dynamic_slice(query, (qblock * TILE, cblock * COL_DEV, zero, zero), (TILE, COL_DEV, H, DH)).astype(jnp.float32)
        keys = lax.dynamic_slice(key, (zero, cblock * COL_DEV, zero, zero), (N, COL_DEV, H, DH)).astype(jnp.float32)
        values = lax.dynamic_slice(value, (zero, cblock * COL_DEV, zero, zero), (N, COL_DEV, H, DH)).astype(jnp.float32)
        scores = jnp.einsum('ijhd,kjhd->jhik', queries, keys)
        bias_part = lax.dynamic_slice(bias, (zero, qblock * TILE, zero), (H, TILE, N)).astype(jnp.float32)
        chain_rows = lax.dynamic_slice(chain_ids, (qblock * TILE,), (TILE,))
        cross = (chain_rows[:, None] != chain_ids[None, :]).astype(jnp.float32)
        scores = scores + bias_part[None] + chain_offset[None, :, None, None] * cross[None, None]
        mask_row = lax.dynamic_slice(tile_mask, (qblock, zero), (1, NB))[0]
        allowed = (jnp.repeat(mask_row, TILE) == 1)[None, None, None, :]
        scores = jnp.where(allowed, scores, -1e+30)
        peak = lax.optimization_barrier(jnp.max(scores, -1, keepdims=True))
        expo = jnp.where(allowed, jnp.exp(scores - peak), 0.0)
        total = lax.optimization_barrier(jnp.sum(expo, -1))
        rounded = lax.optimization_barrier(expo.astype(jnp.bfloat16)).astype(jnp.float32)
        summed = jnp.einsum('jhik,kjhd->ijhd', rounded, values)
        return summed / jnp.transpose(total, (2, 0, 1))[..., None]
    blocks = lax.map(attend_block, flat)
    blocks = blocks.reshape(NB, col_blocks, TILE, COL_DEV, H, DH)
    attended = jnp.transpose(blocks, (0, 2, 1, 3, 4, 5)).reshape(N * COLS, HD)
    gated = (gate * attended).astype(jnp.bfloat16)
    update = jnp.dot(gated, w_out, preferred_element_type=jnp.float32) + out_bias
    return update.astype(jnp.bfloat16).reshape(N, COLS, C)
```

```python
import functools
import math

import jax
import jax.numpy as jnp
from jax import lax
from jax.experimental import pallas as pl
from jax.experimental.pallas import tpu as pltpu
from jax.sharding import PartitionSpec as P

H = 4
DH = 32
TILE = 128
HD = 128
COLS = 4
NB = 16
NSEL = 8
HALF = 256
LOG2E = math.log2(math.e)
MESH = pl.DeviceIdType.MESH
F32 = jnp.float32
BF16 = jnp.bfloat16

BIAS_IDS = ["A+1", "A-1", "A+2", "A-2", "A+3", "A-3", "A4", "B0", "B+1", "B-1", "B+2", "B-2", "B+3", "B-3", "B4"]
NORM_IDS = ["P+1", "P-1", "P2", "Q0", "Q+1", "Q-1", "Q2"]
SIB_IDS = ["P0"] + NORM_IDS


def nt(a, b):
    return lax.dot_general(a, b, (((1,), (1,)), ((), ())), preferred_element_type=F32)


def nn(a, b):
    return jnp.dot(a, b, preferred_element_type=F32)


def kernel(
    mask_ref,
    offset_ref,
    pair_ref,
    gain_ref,
    shift_ref,
    wq_ref,
    wk_ref,
    wv_ref,
    wg_ref,
    gb_ref,
    wo_ref,
    ob_ref,
    bias_ref,
    chain_ref,
    out_ref,
    bias_all,
    norm_all,
    rows_f32,
    qp_ref,
    gate_ref,
    bx_ref,
    s_ref,
    bias_send,
    bias_recv,
    norm_send,
    norm_recv,
    sib_send,
    sib_recv,
    local_sem,
):
    r = lax.axis_index("row")
    c = lax.axis_index("col")
    core, yh, x = r % 2, (r // 2) % 2, r // 4
    z, yl = c % 8, c // 8

    def row_of(dx, flip):
        return ((x + dx + 4) % 4) * 4 + ((yh + flip) % 2) * 2 + core

    def col_of(dz, flip):
        return ((yl + flip) % 2) * 8 + (z + dz + 8) % 8

    up = (r, col_of(1, 0))
    down = (r, col_of(-1, 0))
    across = (r, col_of(0, 1))
    right = (row_of(1, 0), c)
    left = (row_of(-1, 0), c)
    far = (row_of(0, 1), c)
    sib_row = r + 1 - 2 * core
    sib = (sib_row, c)

    barrier = pltpu.get_barrier_semaphore()
    for peer in (up, down, across, right, left, far, sib):
        pl.semaphore_signal(barrier, inc=1, device_id=peer, device_id_type=MESH)

    values = pair_ref[...].astype(F32)
    center = values - jnp.mean(values, -1, keepdims=True)
    spread = jnp.mean(center * center, -1, keepdims=True)
    rows_f32[...] = center * lax.rsqrt(spread + 1e-05) * gain_ref[...] + shift_ref[...]
    for j in range(COLS):
        norm_all[r, j // 2, (j % 2) * TILE:(j % 2 + 1) * TILE, :] = rows_f32[
            pl.ds(j, TILE, stride=COLS), :
        ].astype(BF16)

    pl.semaphore_wait(barrier, 7)

    sends = []

    def bias_slot(name):
        flip = 0 if name[0] == "A" else 1
        dist = int(name[1:])
        return col_of(-dist, flip)

    def norm_slot(name, base=None):
        flip = 0 if name[0] == "P" else 1
        dist = int(name[1:])
        return row_of(-dist, flip)

    def send_bias(src_name, p, peer, as_name):
        if src_name == "A0":
            src = bias_ref.at[p]
        else:
            src = bias_all.at[bias_slot(src_name), p]
        copy = pltpu.make_async_remote_copy(
            src_ref=src,
            dst_ref=bias_all.at[bias_slot(src_name), p],
            send_sem=bias_send.at[len([s for s in sends if s[0] == "b"])],
            recv_sem=bias_recv.at[BIAS_IDS.index(as_name) * 2 + p],
            device_id=peer,
            device_id_type=MESH,
        )
        copy.start()
        sends.append(("b", copy))

    def wait_bias(name, p):
        ref = bias_all.at[bias_slot(name), p]
        sem = bias_recv.at[BIAS_IDS.index(name) * 2 + p]
        pltpu.make_async_remote_copy(
            src_ref=ref, dst_ref=ref, send_sem=bias_send.at[0], recv_sem=sem, device_id=up, device_id_type=MESH
        ).wait_recv()

    def send_norm(src_name, p, peer, as_name):
        slot = norm_slot(src_name)
        copy = pltpu.make_async_remote_copy(
            src_ref=norm_all.at[slot, p],
            dst_ref=norm_all.at[slot, p],
            send_sem=norm_send.at[len([s for s in sends if s[0] == "n"])],
            recv_sem=norm_recv.at[NORM_IDS.index(as_name) * 2 + p],
            device_id=peer,
            device_id_type=MESH,
        )
        copy.start()
        sends.append(("n", copy))

    def wait_norm(name, p):
        ref = norm_all.at[norm_slot(name), p]
        sem = norm_recv.at[NORM_IDS.index(name) * 2 + p]
        pltpu.make_async_remote_copy(
            src_ref=ref, dst_ref=ref, send_sem=norm_send.at[0], recv_sem=sem, device_id=up, device_id_type=MESH
        ).wait_recv()

    def send_sib(name):
        slot = norm_slot(name)
        copy = pltpu.make_async_remote_copy(
            src_ref=norm_all.at[slot],
            dst_ref=norm_all.at[slot],
            send_sem=sib_send.at[SIB_IDS.index(name)],
            recv_sem=sib_recv.at[SIB_IDS.index(name)],
            device_id=sib,
            device_id_type=MESH,
        )
        copy.start()
        sends.append(("s", copy))

    def wait_sib(name):
        ref = norm_all.at[norm_slot(name) + 1 - 2 * core]
        index = SIB_IDS.index(name)
        pltpu.make_async_remote_copy(
            src_ref=ref,
            dst_ref=ref,
            send_sem=sib_send.at[index],
            recv_sem=sib_recv.at[index],
            device_id=sib,
            device_id_type=MESH,
        ).wait_recv()

    for p in range(2):
        send_bias("A0", p, up, "A+1")
        send_bias("A0", p, down, "A-1")
        send_bias("A0", p, across, "B0")
        send_norm("P0", p, right, "P+1")
        send_norm("P0", p, left, "P-1")
        send_norm("P0", p, far, "Q0")
    send_sib("P0")
    own = pltpu.make_async_copy(bias_ref, bias_all.at[c], local_sem)
    own.start()

    mine = norm_all[r].reshape(COLS * TILE, HD)
    query = (nn(mine, wq_ref[...]) * (1.0 / DH**0.5)).astype(BF16)
    gate_ref[...] = jax.nn.sigmoid(nn(mine, wg_ref[...]) + gb_ref[...])
    head = lax.broadcasted_iota(jnp.int32, (TILE, HD), 1) // DH
    for j in range(COLS):
        part = query[j * TILE:(j + 1) * TILE]
        stacked = jnp.concatenate([jnp.where(head == h, part, jnp.zeros_like(part)) for h in range(H)], axis=0)
        qp_ref[j] = (nt(stacked, wk_ref[...]) * LOG2E).astype(BF16)

    picks = [jnp.int32(0) for _ in range(NSEL)]
    count = jnp.int32(0)
    for k in range(NB):
        flag = mask_ref[r, k]
        for n in range(NSEL):
            picks[n] = jnp.where((flag == 1) & (count == n), k, picks[n])
        count = count + jnp.where(flag == 1, 1, 0)
    pads = [jnp.where(n < count, 0.0, -1e30).astype(F32) for n in range(NSEL)]

    for p in range(2):
        wait_bias("A+1", p)
        send_bias("A+1", p, up, "A+2")
        wait_bias("A-1", p)
        send_bias("A-1", p, down, "A-2")
        wait_bias("B0", p)
        send_bias("B0", p, up, "B+1")
        send_bias("B0", p, down, "B-1")
        wait_norm("P+1", p)
        if p == 0:
            send_norm("P+1", p, right, "P2")
        wait_norm("P-1", p)
        if p == 1:
            send_norm("P-1", p, left, "P2")
        wait_norm("Q0", p)
        send_norm("Q0", p, right, "Q+1")
        send_norm("Q0", p, left, "Q-1")
    for name in ("P+1", "P-1", "Q0"):
        send_sib(name)
    for p in range(2):
        wait_bias("A+2", p)
        send_bias("A+2", p, up, "A+3")
        send_bias("A+2", p, across, "B+2")
        wait_bias("A-2", p)
        send_bias("A-2", p, down, "A-3")
        send_bias("A-2", p, across, "B-2")
    for p in range(2):
        wait_norm("Q+1", p)
        if p == 0:
            send_norm("Q+1", p, right, "Q2")
        wait_norm("Q-1", p)
        if p == 1:
            send_norm("Q-1", p, left, "Q2")
    wait_norm("P2", 0)
    wait_norm("P2", 1)
    for name in ("P2", "Q+1", "Q-1"):
        send_sib(name)
    for p in range(2):
        wait_bias("B+2", p)
        send_bias("B+2", p, up, "B+3")
        wait_bias("B-2", p)
        send_bias("B-2", p, down, "B-3")
        wait_bias("A+3", p)
        if p == 0:
            send_bias("A+3", p, up, "A4")
        wait_bias("A-3", p)
        if p == 1:
            send_bias("A-3", p, down, "A4")
    wait_norm("Q2", 0)
    wait_norm("Q2", 1)
    send_sib("Q2")
    for p in range(2):
        wait_bias("A4", p)
        send_bias("A4", p, across, "B4")
    for name in ("B+1", "B-1", "B+3", "B-3", "B4"):
        for p in range(2):
            wait_bias(name, p)
    for name in SIB_IDS:
        wait_sib(name)
    own.wait()

    chain_i = jnp.transpose(jnp.broadcast_to(chain_ref[pl.ds(r, 1), :], (TILE, TILE)))
    for n in range(NSEL):
        chain_k = chain_ref[pl.ds(picks[n], 1), :]
        differs = chain_i != chain_k
        for h in range(H):
            part = bias_all[picks[n], h // 2, (h % 2) * TILE:(h % 2 + 1) * TILE, :].astype(F32)
            total = part + jnp.where(differs, offset_ref[h], 0.0) + pads[n]
            bx_ref[n // 2, h * TILE:(h + 1) * TILE, (n % 2) * TILE:(n % 2 + 1) * TILE] = total * LOG2E

    for j in range(COLS):
        keys = [
            jnp.concatenate(
                [
                    norm_all[picks[2 * m + e], j // 2, (j % 2) * TILE:(j % 2 + 1) * TILE, :]
                    for e in range(2)
                ],
                axis=0,
            )
            for m in range(NSEL // 2)
        ]
        queries = qp_ref[j]
        peak = None
        for m in range(NSEL // 2):
            scores = nt(queries, keys[m]) + bx_ref[m]
            s_ref[m] = scores
            best = jnp.maximum(scores[:, :TILE], scores[:, TILE:])
            peak = best if peak is None else jnp.maximum(peak, best)
        peak = jnp.max(peak, axis=-1, keepdims=True)
        total, summed = None, None
        for m in range(NSEL // 2):
            expo = jnp.exp2(s_ref[m] - peak)
            part = expo[:, :TILE] + expo[:, TILE:]
            total = part if total is None else total + part
            prod = nn(expo.astype(BF16), keys[m])
            summed = prod if summed is None else summed + prod
        total = jnp.sum(total, axis=-1, keepdims=True)
        mixed = summed / total
        high = mixed.astype(BF16)
        low = (mixed - high.astype(F32)).astype(BF16)
        heads = nn(high, wv_ref[...]) + nn(low, wv_ref[...])
        attended = jnp.where(head == 0, heads[:TILE], 0.0)
        for h in range(1, H):
            attended = jnp.where(head == h, heads[h * TILE:(h + 1) * TILE], attended)
        gated = (gate_ref[j * TILE:(j + 1) * TILE, :] * attended).astype(BF16)
        rows_f32[pl.ds(j, TILE, stride=COLS), :] = nn(gated, wo_ref[...]) + ob_ref[...]
    out_ref[...] = rows_f32[...].astype(BF16)

    for _, copy in sends:
        copy.wait_send()


def on_device(
    pair,
    norm_gain,
    norm_offset,
    w_query,
    w_key,
    w_value,
    w_gate,
    gate_bias,
    w_out,
    out_bias,
    bias,
    chain_offset,
    chain_ids,
    tile_mask,
):
    smem = pl.BlockSpec(memory_space=pltpu.SMEM)
    vmem = pl.BlockSpec(memory_space=pltpu.VMEM)
    hbm = pl.BlockSpec(memory_space=pl.ANY)
    out = pl.pallas_call(
        kernel,
        out_shape=jax.ShapeDtypeStruct((TILE * COLS, HD), BF16),
        in_specs=[smem, smem] + [vmem] * 10 + [hbm, vmem],
        out_specs=vmem,
        scratch_shapes=[
            pltpu.VMEM((NB, 2, HALF, TILE), BF16),
            pltpu.VMEM((NB, 2, HALF, HD), BF16),
            pltpu.VMEM((TILE * COLS, HD), F32),
            pltpu.VMEM((COLS, H * TILE, HD), BF16),
            pltpu.VMEM((COLS * TILE, HD), F32),
            pltpu.VMEM((NSEL // 2, H * TILE, 2 * TILE), F32),
            pltpu.VMEM((NSEL // 2, H * TILE, 2 * TILE), F32),
            pltpu.SemaphoreType.DMA((32,)),
            pltpu.SemaphoreType.DMA((30,)),
            pltpu.SemaphoreType.DMA((14,)),
            pltpu.SemaphoreType.DMA((14,)),
            pltpu.SemaphoreType.DMA((8,)),
            pltpu.SemaphoreType.DMA((8,)),
            pltpu.SemaphoreType.DMA,
        ],
        compiler_params=pltpu.CompilerParams(
            collective_id=0, has_side_effects=True, vmem_limit_bytes=48 * 1024 * 1024
        ),
        cost_estimate=pl.CostEstimate(flops=1 << 30, bytes_accessed=1 << 20, transcendentals=1 << 21),
    )(
        tile_mask,
        chain_offset,
        pair.reshape(TILE * COLS, HD),
        norm_gain.reshape(1, HD),
        norm_offset.reshape(1, HD),
        w_query,
        w_key,
        w_value,
        w_gate,
        gate_bias.reshape(1, HD),
        w_out,
        out_bias.reshape(1, HD),
        bias.reshape(2, HALF, TILE),
        chain_ids.reshape(NB, TILE),
    )
    return out.reshape(TILE, COLS, HD)


def solution(mesh):
    placed = (
        P("row", "col", None),
        P(),
        P(),
        P(),
        P(),
        P(),
        P(),
        P(),
        P(),
        P(),
        P(None, "row", "col"),
        P(),
        P(),
        P(),
    )
    return jax.shard_map(
        on_device, mesh=mesh, in_specs=placed, out_specs=P("row", "col", None), check_vma=False
    )
```

```python
import functools
import math

import jax
import jax.numpy as jnp
from jax import lax
from jax.experimental import pallas as pl
from jax.experimental.pallas import tpu as pltpu
from jax.sharding import PartitionSpec as P

H = 4
DH = 32
TILE = 128
HD = 128
COLS = 4
NB = 16
NSEL = 8
SLICE = 32
DEPTH = NSEL * TILE
LOG2E = math.log2(math.e)
MESH = pl.DeviceIdType.MESH
F32 = jnp.float32
BF16 = jnp.bfloat16

BIAS_IDS = ["A+1", "A-1", "A+2", "A-2", "A+3", "A-3", "A4", "B0", "B+1", "B-1", "B+2", "B-2", "B+3", "B-3", "B4"]
NORM_IDS = ["P+1", "P-1", "P2", "Q0", "Q+1", "Q-1", "Q2"]
SIB_IDS = ["P0"] + NORM_IDS
EARLY = ["A+0", "A+1", "A-1", "B0", "B+1", "B-1", "A+2", "A-2"]
LATE = ["B+2", "B-2", "A+3", "A-3", "A4", "B+3", "B-3", "B4"]


def nt(a, b):
    return lax.dot_general(a, b, (((1,), (1,)), ((), ())), preferred_element_type=F32)


def nn(a, b):
    return jnp.dot(a, b, preferred_element_type=F32)


def kernel(
    pair_in,
    gain_in,
    shift_in,
    wq_in,
    wk_in,
    wv_in,
    wg_in,
    gb_in,
    bias_ref,
    offset_in,
    chain_in,
    mask_in,
    out_ref,
    pair_ref,
    gain_ref,
    shift_ref,
    wq_ref,
    wk_ref,
    wv_ref,
    wg_ref,
    gb_ref,
    offset_ref,
    chain_ref,
    mask_ref,
    slices_ref,
    bias_all,
    norm_0,
    norm_1,
    rows_f32,
    qp_ref,
    gate_ref,
    chain_i_ref,
    s_ref,
    p_ref,
    o_ref,
    swap_send,
    swap_recv,
    bias_send,
    bias_recv,
    norm_send,
    norm_recv,
    sib_send,
    sib_recv,
    in_sem,
):
    r = lax.axis_index("row")
    c = lax.axis_index("col")
    core, yh, x = r % 2, (r // 2) % 2, r // 4
    z, yl = c % 8, c // 8
    norm_refs = (norm_0, norm_1)

    def row_of(dx, flip):
        return ((x + dx + 4) % 4) * 4 + ((yh + flip) % 2) * 2 + core

    def col_of(dz, flip):
        return ((yl + flip) % 2) * 8 + (z + dz + 8) % 8

    up = (r, col_of(1, 0))
    down = (r, col_of(-1, 0))
    across = (r, col_of(0, 1))
    right = (row_of(1, 0), c)
    left = (row_of(-1, 0), c)
    far = (row_of(0, 1), c)
    sib = (r + 1 - 2 * core, c)

    moves = [
        pltpu.make_async_copy(src, dst, in_sem.at[i])
        for i, (src, dst) in enumerate(
            (
                (pair_in, pair_ref),
                (gain_in, gain_ref),
                (shift_in, shift_ref),
                (wq_in, wq_ref),
                (wg_in, wg_ref),
                (gb_in, gb_ref),
                (wk_in, wk_ref),
                (mask_in, mask_ref),
                (offset_in, offset_ref),
                (chain_in, chain_ref),
                (wv_in, wv_ref),
                (bias_ref.at[pl.ds(c * SLICE, SLICE)], slices_ref.at[c]),
            )
        )
    ]
    for move in moves:
        move.start()

    swaps = [(flip * 8 + dz, (r, col_of(dz, flip))) for flip in range(2) for dz in range(8) if flip or dz]
    barrier = pltpu.get_barrier_semaphore()
    for peer in [peer for _, peer in swaps] + [right, left, far, sib]:
        pl.semaphore_signal(barrier, inc=1, device_id=peer, device_id_type=MESH)
    pl.semaphore_wait(barrier, 19)

    sends = []

    for index, peer in swaps:
        copy = pltpu.make_async_remote_copy(
            src_ref=bias_ref.at[pl.ds(peer[1] * SLICE, SLICE)],
            dst_ref=slices_ref.at[c],
            send_sem=swap_send.at[index],
            recv_sem=swap_recv.at[index],
            device_id=peer,
            device_id_type=MESH,
        )
        copy.start()
        sends.append(("w", copy))

    def wait_swaps():
        for index, _ in swaps:
            ref = slices_ref.at[col_of(-(index % 8), index // 8)]
            pltpu.make_async_remote_copy(
                src_ref=ref,
                dst_ref=ref,
                send_sem=swap_send.at[index],
                recv_sem=swap_recv.at[index],
                device_id=up,
                device_id_type=MESH,
            ).wait_recv()

    def bias_slot(name):
        return col_of(-int(name[1:]), 0 if name[0] == "A" else 1)

    def norm_slot(name):
        return row_of(-int(name[1:]), 0 if name[0] == "P" else 1)

    def send_bias(src_name, p, peer, as_name):
        ref = bias_all.at[bias_slot(src_name), pl.ds(p * 4, 4)]
        copy = pltpu.make_async_remote_copy(
            src_ref=ref,
            dst_ref=ref,
            send_sem=bias_send.at[len([s for s in sends if s[0] == "b"])],
            recv_sem=bias_recv.at[BIAS_IDS.index(as_name) * 2 + p],
            device_id=peer,
            device_id_type=MESH,
        )
        copy.start()
        sends.append(("b", copy))

    def wait_bias(name, p):
        ref = bias_all.at[bias_slot(name), pl.ds(p * 4, 4)]
        sem = bias_recv.at[BIAS_IDS.index(name) * 2 + p]
        pltpu.make_async_remote_copy(
            src_ref=ref, dst_ref=ref, send_sem=bias_send.at[0], recv_sem=sem, device_id=up, device_id_type=MESH
        ).wait_recv()

    def norm_part(name, p, e):
        ref = norm_refs[p].at[norm_slot(name)]
        return ref if e is None else ref.at[e]

    def norm_sem(name, p, e):
        return norm_recv.at[(NORM_IDS.index(name) * 2 + p) * 2 + (0 if e is None else e)]

    def send_norm(src_name, p, e, peer, as_name):
        ref = norm_part(src_name, p, e)
        copy = pltpu.make_async_remote_copy(
            src_ref=ref,
            dst_ref=ref,
            send_sem=norm_send.at[len([s for s in sends if s[0] == "n"])],
            recv_sem=norm_sem(as_name, p, e),
            device_id=peer,
            device_id_type=MESH,
        )
        copy.start()
        sends.append(("n", copy))

    def wait_norm(name, p, e=None):
        ref = norm_part(name, p, e)
        pltpu.make_async_remote_copy(
            src_ref=ref,
            dst_ref=ref,
            send_sem=norm_send.at[0],
            recv_sem=norm_sem(name, p, e),
            device_id=up,
            device_id_type=MESH,
        ).wait_recv()

    def send_sib(name, p):
        ref = norm_refs[p].at[norm_slot(name)]
        index = SIB_IDS.index(name) * 2 + p
        copy = pltpu.make_async_remote_copy(
            src_ref=ref,
            dst_ref=ref,
            send_sem=sib_send.at[index],
            recv_sem=sib_recv.at[index],
            device_id=sib,
            device_id_type=MESH,
        )
        copy.start()
        sends.append(("s", copy))

    def wait_sibs(p):
        for i, name in enumerate(SIB_IDS):
            ref = norm_refs[p].at[norm_slot(name) + 1 - 2 * core]
            pltpu.make_async_remote_copy(
                src_ref=ref,
                dst_ref=ref,
                send_sem=sib_send.at[i * 2 + p],
                recv_sem=sib_recv.at[i * 2 + p],
                device_id=sib,
                device_id_type=MESH,
            ).wait_recv()

    for move in moves[:3]:
        move.wait()
    values = pair_ref[...].astype(F32)
    center = values - jnp.mean(values, -1, keepdims=True)
    spread = jnp.mean(center * center, -1, keepdims=True)
    rows_f32[...] = center * lax.rsqrt(spread + 1e-05) * gain_ref[...] + shift_ref[...]
    for p in range(2):
        for e in range(2):
            norm_refs[p][r, e] = rows_f32[pl.ds(2 * p + e, TILE, stride=COLS), :].astype(BF16)
        send_norm("P0", p, None, right, "P+1")
        send_norm("P0", p, None, left, "P-1")
        send_norm("P0", p, None, far, "Q0")
        send_sib("P0", p)
    for move in moves[3:]:
        move.wait()

    picks = [jnp.int32(0) for _ in range(NSEL)]
    count = jnp.int32(0)
    for k in range(NB):
        flag = mask_ref[r, k]
        for n in range(NSEL):
            picks[n] = jnp.where((flag == 1) & (count == n), k, picks[n])
        count = count + jnp.where(flag == 1, 1, 0)
    pads = [jnp.where(n < count, 0.0, -1e30).astype(F32) for n in range(NSEL)]

    mine = jnp.concatenate([norm_refs[p][r].reshape(2 * TILE, HD) for p in range(2)], axis=0)
    query = (nn(mine, wq_ref[...]) * (1.0 / DH**0.5)).astype(BF16)
    head = lax.broadcasted_iota(jnp.int32, (TILE, HD), 1) // DH
    for j in range(COLS):
        part = query[j * TILE:(j + 1) * TILE]
        stacked = jnp.concatenate([jnp.where(head == h, part, jnp.zeros_like(part)) for h in range(H)], axis=0)
        qp_ref[j] = (nt(stacked, wk_ref[...]) * LOG2E).astype(BF16)

    wait_swaps()
    for n in range(NSEL):
        bias_all[c, n] = slices_ref[picks[n]]
    for p in range(2):
        send_bias("A0", p, up, "A+1")
        send_bias("A0", p, down, "A-1")
        send_bias("A0", p, across, "B0")

    gate_ref[...] = jax.nn.sigmoid(nn(mine, wg_ref[...]) + gb_ref[...])
    chain_i_ref[...] = jnp.transpose(jnp.broadcast_to(chain_ref[pl.ds(r, 1), :], (TILE, TILE)))

    for p in range(2):
        wait_norm("P+1", p)
        send_norm("P+1", p, 0, right, "P2")
        wait_norm("P-1", p)
        send_norm("P-1", p, 1, left, "P2")
        wait_norm("Q0", p)
        send_norm("Q0", p, None, right, "Q+1")
        send_norm("Q0", p, None, left, "Q-1")
        for name in ("P+1", "P-1", "Q0"):
            send_sib(name, p)
    for p in range(2):
        wait_bias("A+1", p)
        send_bias("A+1", p, up, "A+2")
        wait_bias("A-1", p)
        send_bias("A-1", p, down, "A-2")
        wait_bias("B0", p)
        send_bias("B0", p, up, "B+1")
        send_bias("B0", p, down, "B-1")
    for p in range(2):
        for name in ("Q+1", "Q-1"):
            wait_norm(name, p)
        send_norm("Q+1", p, 0, right, "Q2")
        send_norm("Q-1", p, 1, left, "Q2")
        wait_norm("P2", p, 0)
        wait_norm("P2", p, 1)
        for name in ("Q+1", "Q-1", "P2"):
            send_sib(name, p)
    for p in range(2):
        wait_bias("A+2", p)
        send_bias("A+2", p, up, "A+3")
        send_bias("A+2", p, across, "B+2")
        wait_bias("A-2", p)
        send_bias("A-2", p, down, "A-3")
        send_bias("A-2", p, across, "B-2")

    def keys_of(j, m):
        return jnp.concatenate([norm_refs[j // 2][picks[2 * m + e], j % 2] for e in range(2)], axis=0)

    def score(p):
        for j in range(2 * p, 2 * p + 2):
            queries = qp_ref[j]
            for m in range(NSEL // 2):
                s_ref[j, :, 2 * m * TILE:2 * (m + 1) * TILE] = nt(queries, keys_of(j, m))

    def finish_norm(p):
        wait_norm("Q2", p, 0)
        wait_norm("Q2", p, 1)
        send_sib("Q2", p)
        wait_sibs(p)

    finish_norm(0)
    score(0)
    for p in range(2):
        wait_bias("B+2", p)
        send_bias("B+2", p, up, "B+3")
        wait_bias("B-2", p)
        send_bias("B-2", p, down, "B-3")
        wait_bias("A+3", p)
        if p == 0:
            send_bias("A+3", p, up, "A4")
        wait_bias("A-3", p)
        if p == 1:
            send_bias("A-3", p, down, "A4")
    finish_norm(1)
    for p in range(2):
        wait_bias("A4", p)
        send_bias("A4", p, across, "B4")
    score(1)

    def softmax(batch, t, name):
        slot = bias_slot(name)
        rows = pl.ds(pl.multiple_of(slot * SLICE, SLICE), SLICE)
        chain_i = chain_i_ref[pl.ds(pl.multiple_of((slot % 4) * SLICE, SLICE), SLICE), :]
        extra = offset_ref[slot // 4]
        parts = []
        for n in range(NSEL):
            differs = chain_i != chain_ref[pl.ds(picks[n], 1), :]
            parts.append((bias_all[slot, n].astype(F32) + jnp.where(differs, extra, 0.0) + pads[n]) * LOG2E)
        bias = jnp.concatenate(parts, axis=1)
        inverse = []
        for j in range(COLS):
            scores = s_ref[j, rows, :] + bias
            expo = jnp.exp2(scores - jnp.max(scores, axis=-1, keepdims=True))
            inverse.append(1.0 / jnp.sum(expo, axis=-1, keepdims=True))
            p_ref[batch, j, t * SLICE:(t + 1) * SLICE, :] = expo.astype(BF16)
        return rows, inverse

    def mix(batch, done):
        for j in range(COLS):
            keys = jnp.concatenate([keys_of(j, m) for m in range(NSEL // 2)], axis=0)
            summed = nn(p_ref[batch, j], keys)
            for t, (rows, inverse) in enumerate(done):
                o_ref[j, rows, :] = summed[t * SLICE:(t + 1) * SLICE] * inverse[j]

    for name in ("B+1", "B-1"):
        for p in range(2):
            wait_bias(name, p)
    done = [softmax(0, t, name) for t, name in enumerate(EARLY)]
    mix(0, done)
    for name in ("B+3", "B-3", "B4"):
        for p in range(2):
            wait_bias(name, p)
    done = [softmax(1, t, name) for t, name in enumerate(LATE)]
    mix(1, done)

    for j in range(COLS):
        mixed = o_ref[j]
        high = mixed.astype(BF16)
        low = (mixed - high.astype(F32)).astype(BF16)
        heads = nn(high, wv_ref[...]) + nn(low, wv_ref[...])
        attended = jnp.where(head == 0, heads[:TILE], 0.0)
        for h in range(1, H):
            attended = jnp.where(head == h, heads[h * TILE:(h + 1) * TILE], attended)
        rows_f32[pl.ds(j, TILE, stride=COLS), :] = gate_ref[j * TILE:(j + 1) * TILE, :] * attended
    out_ref[...] = rows_f32[...].astype(BF16)

    for _, copy in sends:
        copy.wait_send()


def on_device(
    pair,
    norm_gain,
    norm_offset,
    w_query,
    w_key,
    w_value,
    w_gate,
    gate_bias,
    w_out,
    out_bias,
    bias,
    chain_offset,
    chain_ids,
    tile_mask,
):
    hbm = pl.BlockSpec(memory_space=pltpu.HBM)
    vector = pltpu.VMEM((1, HD), F32)
    matrix = pltpu.VMEM((HD, HD), BF16)
    gated = pl.pallas_call(
        kernel,
        out_shape=jax.ShapeDtypeStruct((TILE * COLS, HD), BF16),
        in_specs=[hbm] * 12,
        out_specs=pl.BlockSpec(memory_space=pltpu.VMEM),
        scratch_shapes=[
            pltpu.VMEM((TILE * COLS, HD), BF16),
            vector,
            vector,
            matrix,
            matrix,
            matrix,
            matrix,
            vector,
            pltpu.SMEM((H,), F32),
            pltpu.VMEM((NB, TILE), jnp.int32),
            pltpu.SMEM((NB, NB), jnp.int32),
            pltpu.VMEM((NB, SLICE, TILE), BF16),
            pltpu.VMEM((NB, NSEL, SLICE, TILE), BF16),
            pltpu.VMEM((NB, 2, TILE, HD), BF16),
            pltpu.VMEM((NB, 2, TILE, HD), BF16),
            pltpu.VMEM((TILE * COLS, HD), F32),
            pltpu.VMEM((COLS, H * TILE, HD), BF16),
            pltpu.VMEM((COLS * TILE, HD), F32),
            pltpu.VMEM((TILE, TILE), jnp.int32),
            pltpu.VMEM((COLS, H * TILE, DEPTH), F32),
            pltpu.VMEM((2, COLS, 8 * SLICE, DEPTH), BF16),
            pltpu.VMEM((COLS, H * TILE, HD), F32),
            pltpu.SemaphoreType.DMA((16,)),
            pltpu.SemaphoreType.DMA((16,)),
            pltpu.SemaphoreType.DMA((32,)),
            pltpu.SemaphoreType.DMA((30,)),
            pltpu.SemaphoreType.DMA((20,)),
            pltpu.SemaphoreType.DMA((28,)),
            pltpu.SemaphoreType.DMA((16,)),
            pltpu.SemaphoreType.DMA((16,)),
            pltpu.SemaphoreType.DMA((12,)),
        ],
        compiler_params=pltpu.CompilerParams(
            collective_id=0, has_side_effects=True, vmem_limit_bytes=64 * 1024 * 1024
        ),
        cost_estimate=pl.CostEstimate(flops=1 << 30, bytes_accessed=1 << 20, transcendentals=1 << 21),
    )(
        pair.reshape(TILE * COLS, HD),
        norm_gain.reshape(1, HD),
        norm_offset.reshape(1, HD),
        w_query,
        w_key,
        w_value,
        w_gate,
        gate_bias.reshape(1, HD),
        bias.reshape(H * TILE, TILE),
        chain_offset,
        chain_ids.reshape(NB, TILE),
        tile_mask,
    )
    update = jnp.dot(gated, w_out, preferred_element_type=F32) + out_bias
    return update.astype(BF16).reshape(TILE, COLS, HD)


def solution(mesh):
    placed = (
        P("row", "col", None),
        P(),
        P(),
        P(),
        P(),
        P(),
        P(),
        P(),
        P(),
        P(),
        P(None, "row", "col"),
        P(),
        P(),
        P(),
    )
    return jax.shard_map(
        on_device, mesh=mesh, in_specs=placed, out_specs=P("row", "col", None), check_vma=False
    )
```

```python
import functools
import math

import jax
import jax.numpy as jnp
from jax import lax
from jax.experimental import pallas as pl
from jax.experimental.pallas import tpu as pltpu
from jax.sharding import PartitionSpec as P

H = 4
DH = 32
TILE = 128
HD = 128
COLS = 4
NB = 16
NSEL = 8
SLICE = 32
DEPTH = NSEL * TILE
LOG2E = math.log2(math.e)
MESH = pl.DeviceIdType.MESH
F32 = jnp.float32
BF16 = jnp.bfloat16

BIAS_IDS = ["A+1", "A-1", "A+2", "A-2", "A+3", "A-3", "A4", "B0", "B+1", "B-1", "B+2", "B-2", "B+3", "B-3", "B4"]
NORM_IDS = ["P+1", "P-1", "P2", "Q0", "Q+1", "Q-1", "Q2"]
SIB_IDS = ["P0"] + NORM_IDS
EARLY = ["A+0", "A+1", "A-1", "B0", "B+1", "B-1", "A+2", "A-2"]
LATE = ["B+2", "B-2", "A+3", "A-3", "A4", "B+3", "B-3", "B4"]


def nt(a, b):
    return lax.dot_general(a, b, (((1,), (1,)), ((), ())), preferred_element_type=F32)


def nn(a, b):
    return jnp.dot(a, b, preferred_element_type=F32)


def kernel(
    pair_in,
    gain_in,
    shift_in,
    wq_in,
    wk_in,
    wv_in,
    wg_in,
    gb_in,
    bias_ref,
    offset_in,
    chain_in,
    mask_in,
    out_ref,
    pair_ref,
    gain_ref,
    shift_ref,
    wq_ref,
    wk_ref,
    wv_ref,
    wg_ref,
    gb_ref,
    offset_ref,
    chain_ref,
    mask_ref,
    slices_ref,
    bias_all,
    norm_0,
    norm_1,
    rows_f32,
    qp_ref,
    gate_ref,
    chain_i_ref,
    bx_ref,
    s_ref,
    p_ref,
    o_ref,
    swap_send,
    swap_recv,
    bias_send,
    bias_recv,
    norm_send,
    norm_recv,
    sib_send,
    sib_recv,
    in_sem,
):
    r = lax.axis_index("row")
    c = lax.axis_index("col")
    core, yh, x = r % 2, (r // 2) % 2, r // 4
    z, yl = c % 8, c // 8
    norm_refs = (norm_0, norm_1)

    def row_of(dx, flip):
        return ((x + dx + 4) % 4) * 4 + ((yh + flip) % 2) * 2 + core

    def col_of(dz, flip):
        return ((yl + flip) % 2) * 8 + (z + dz + 8) % 8

    up = (r, col_of(1, 0))
    down = (r, col_of(-1, 0))
    across = (r, col_of(0, 1))
    right = (row_of(1, 0), c)
    left = (row_of(-1, 0), c)
    far = (row_of(0, 1), c)
    up2 = (r, col_of(2, 0))
    down2 = (r, col_of(-2, 0))
    opposite = (row_of(2, 0), c)
    sib = (r + 1 - 2 * core, c)

    moves = [
        pltpu.make_async_copy(src, dst, in_sem.at[i])
        for i, (src, dst) in enumerate(
            (
                (pair_in, pair_ref),
                (gain_in, gain_ref),
                (shift_in, shift_ref),
                (wq_in, wq_ref),
                (wg_in, wg_ref),
                (gb_in, gb_ref),
                (wk_in, wk_ref),
                (mask_in, mask_ref),
                (offset_in, offset_ref),
                (chain_in, chain_ref),
                (wv_in, wv_ref),
                (bias_ref.at[pl.ds(c * SLICE, SLICE)], slices_ref.at[c]),
            )
        )
    ]
    for move in moves:
        move.start()

    swaps = [(flip * 8 + dz, (r, col_of(dz, flip))) for dz in (4, 3, 5, 2, 6, 1, 7, 0) for flip in (1, 0) if flip or dz]
    barrier = pltpu.get_barrier_semaphore()
    for peer in [peer for _, peer in swaps] + [right, left, far, sib, opposite]:
        pl.semaphore_signal(barrier, inc=1, device_id=peer, device_id_type=MESH)

    sends = []

    def wait_swaps():
        for index, _ in swaps:
            ref = slices_ref.at[col_of(-(index % 8), index // 8)]
            pltpu.make_async_remote_copy(
                src_ref=ref,
                dst_ref=ref,
                send_sem=swap_send.at[index],
                recv_sem=swap_recv.at[index],
                device_id=up,
                device_id_type=MESH,
            ).wait_recv()

    def bias_slot(name):
        return col_of(-int(name[1:]), 0 if name[0] == "A" else 1)

    def norm_slot(name):
        return row_of(-int(name[1:]), 0 if name[0] == "P" else 1)

    def send_bias(src_name, p, peer, as_name):
        ref = bias_all.at[bias_slot(src_name), pl.ds(p * 4, 4)]
        copy = pltpu.make_async_remote_copy(
            src_ref=ref,
            dst_ref=ref,
            send_sem=bias_send.at[len([s for s in sends if s[0] == "b"])],
            recv_sem=bias_recv.at[BIAS_IDS.index(as_name) * 2 + p],
            device_id=peer,
            device_id_type=MESH,
        )
        copy.start()
        sends.append(("b", copy))

    def wait_bias(name, p):
        ref = bias_all.at[bias_slot(name), pl.ds(p * 4, 4)]
        sem = bias_recv.at[BIAS_IDS.index(name) * 2 + p]
        pltpu.make_async_remote_copy(
            src_ref=ref, dst_ref=ref, send_sem=bias_send.at[0], recv_sem=sem, device_id=up, device_id_type=MESH
        ).wait_recv()

    def norm_part(name, p, e):
        ref = norm_refs[p].at[norm_slot(name)]
        return ref if e is None else ref.at[e]

    def norm_sem(name, p, e):
        return norm_recv.at[(NORM_IDS.index(name) * 2 + p) * 2 + (0 if e is None else e)]

    def send_norm(src_name, p, e, peer, as_name):
        ref = norm_part(src_name, p, e)
        copy = pltpu.make_async_remote_copy(
            src_ref=ref,
            dst_ref=ref,
            send_sem=norm_send.at[len([s for s in sends if s[0] == "n"])],
            recv_sem=norm_sem(as_name, p, e),
            device_id=peer,
            device_id_type=MESH,
        )
        copy.start()
        sends.append(("n", copy))

    def wait_norm(name, p, e=None):
        ref = norm_part(name, p, e)
        pltpu.make_async_remote_copy(
            src_ref=ref,
            dst_ref=ref,
            send_sem=norm_send.at[0],
            recv_sem=norm_sem(name, p, e),
            device_id=up,
            device_id_type=MESH,
        ).wait_recv()

    def send_sib(name, p):
        ref = norm_refs[p].at[norm_slot(name)]
        index = SIB_IDS.index(name) * 2 + p
        copy = pltpu.make_async_remote_copy(
            src_ref=ref,
            dst_ref=ref,
            send_sem=sib_send.at[index],
            recv_sem=sib_recv.at[index],
            device_id=sib,
            device_id_type=MESH,
        )
        copy.start()
        sends.append(("s", copy))

    def wait_sib(name, p):
        ref = norm_refs[p].at[norm_slot(name) + 1 - 2 * core]
        index = SIB_IDS.index(name) * 2 + p
        pltpu.make_async_remote_copy(
            src_ref=ref,
            dst_ref=ref,
            send_sem=sib_send.at[index],
            recv_sem=sib_recv.at[index],
            device_id=sib,
            device_id_type=MESH,
        ).wait_recv()

    for move in moves[:3]:
        move.wait()
    values = pair_ref[...].astype(F32)
    center = values - jnp.mean(values, -1, keepdims=True)
    spread = jnp.mean(center * center, -1, keepdims=True)
    rows_f32[...] = center * lax.rsqrt(spread + 1e-05) * gain_ref[...] + shift_ref[...]
    for p in range(2):
        for e in range(2):
            norm_refs[p][r, e] = rows_f32[pl.ds(2 * p + e, TILE, stride=COLS), :].astype(BF16)

    pl.semaphore_wait(barrier, 20)
    for p in range(2):
        send_norm("P0", p, None, far, "Q0")
        send_norm("P0", p, None, right, "P+1")
        send_norm("P0", p, None, left, "P-1")

    for index, peer in swaps:
        copy = pltpu.make_async_remote_copy(
            src_ref=bias_ref.at[pl.ds(peer[1] * SLICE, SLICE)],
            dst_ref=slices_ref.at[c],
            send_sem=swap_send.at[index],
            recv_sem=swap_recv.at[index],
            device_id=peer,
            device_id_type=MESH,
        )
        copy.start()
        sends.append(("w", copy))

    for p in range(2):
        send_sib("P0", p)
    for move in moves[3:]:
        move.wait()

    picks = [jnp.int32(0) for _ in range(NSEL)]
    count = jnp.int32(0)
    for k in range(NB):
        flag = mask_ref[r, k]
        for n in range(NSEL):
            picks[n] = jnp.where((flag == 1) & (count == n), k, picks[n])
        count = count + jnp.where(flag == 1, 1, 0)
    pads = [jnp.where(n < count, 0.0, -1e30).astype(F32) for n in range(NSEL)]

    mine = jnp.concatenate([norm_refs[p][r].reshape(2 * TILE, HD) for p in range(2)], axis=0)
    query = (nn(mine, wq_ref[...]) * (1.0 / DH**0.5)).astype(BF16)
    head = lax.broadcasted_iota(jnp.int32, (TILE, HD), 1) // DH
    for j in range(COLS):
        part = query[j * TILE:(j + 1) * TILE]
        stacked = jnp.concatenate([jnp.where(head == h, part, jnp.zeros_like(part)) for h in range(H)], axis=0)
        qp_ref[j] = (nt(stacked, wk_ref[...]) * LOG2E).astype(BF16)

    gate_ref[...] = jax.nn.sigmoid(nn(mine, wg_ref[...]) + gb_ref[...])
    chain_i_ref[...] = jnp.transpose(jnp.broadcast_to(chain_ref[pl.ds(r, 1), :], (TILE, TILE)))

    def keys_of(j, m):
        return jnp.concatenate([norm_refs[j // 2][picks[2 * m + e], j % 2] for e in range(2)], axis=0)

    def score(name, p):
        wait_sib(name, p)
        first = norm_slot(name) - core
        for e in range(2):
            keys = norm_refs[p][pl.ds(first, 2), e].reshape(2 * TILE, HD)
            both = nt(qp_ref[2 * p + e], keys)
            s_ref[2 * p + e, first] = both[:, :TILE]
            s_ref[2 * p + e, first + 1] = both[:, TILE:]

    def pass_first(p):
        wait_norm("Q0", p)
        send_norm("Q0", p, None, right, "Q+1")
        send_norm("Q0", p, None, left, "Q-1")
        send_norm("Q0", p, None, opposite, "Q2")
        wait_norm("P+1", p)
        send_norm("P+1", p, 0, right, "P2")
        wait_norm("P-1", p)
        send_norm("P-1", p, 1, left, "P2")
        for name in ("P+1", "P-1", "Q0"):
            send_sib(name, p)

    def pass_second(p):
        wait_norm("P2", p, 0)
        wait_norm("P2", p, 1)
        for name in ("Q+1", "Q-1"):
            wait_norm(name, p)
        for name in ("P2", "Q+1", "Q-1"):
            send_sib(name, p)

    for p in range(2):
        score("P0", p)
    pass_first(0)
    wait_swaps()
    for n in range(NSEL):
        bias_all[c, n] = slices_ref[picks[n]]
    for p in range(2):
        send_bias("A0", p, up, "A+1")
        send_bias("A0", p, down, "A-1")
        send_bias("A0", p, across, "B0")
    for p in range(2):
        send_bias("A0", p, up2, "A+2")
        send_bias("A0", p, down2, "A-2")
    pass_first(1)
    for name in ("P+1", "P-1", "Q0"):
        score(name, 0)
    for p in range(2):
        wait_bias("A+1", p)
        send_bias("A+1", p, across, "B+1")
        wait_bias("A-1", p)
        send_bias("A-1", p, across, "B-1")
    for name in ("P+1", "P-1", "Q0"):
        score(name, 1)
    pass_second(0)
    for p in range(2):
        wait_bias("A+2", p)
        if p == 0:
            send_bias("A+2", p, up2, "A4")
        send_bias("A+2", p, across, "B+2")
        send_bias("A+2", p, up, "A+3")
        wait_bias("A-2", p)
        if p == 1:
            send_bias("A-2", p, down2, "A4")
        send_bias("A-2", p, across, "B-2")
        send_bias("A-2", p, down, "A-3")
    for name in ("P2", "Q+1", "Q-1"):
        score(name, 0)
    pass_second(1)
    wait_norm("Q2", 0)
    send_sib("Q2", 0)
    for p in range(2):
        wait_bias("B+2", p)
        send_bias("B+2", p, up, "B+3")
        wait_bias("B-2", p)
        send_bias("B-2", p, down, "B-3")
        wait_bias("A4", p)
        send_bias("A4", p, across, "B4")
    wait_norm("Q2", 1)
    send_sib("Q2", 1)
    for name in ("P2", "Q+1", "Q-1"):
        score(name, 1)

    def prepare(batch, t, name):
        slot = bias_slot(name)
        chain_i = chain_i_ref[pl.ds(pl.multiple_of((slot % 4) * SLICE, SLICE), SLICE), :]
        extra = offset_ref[slot // 4]
        for n in range(NSEL):
            differs = chain_i != chain_ref[pl.ds(picks[n], 1), :]
            part = (bias_all[slot, n].astype(F32) + jnp.where(differs, extra, 0.0) + pads[n]) * LOG2E
            bx_ref[batch, t * SLICE:(t + 1) * SLICE, n * TILE:(n + 1) * TILE] = part

    def attend(batch, names, p):
        rows = [pl.ds(pl.multiple_of(bias_slot(name) * SLICE, SLICE), SLICE) for name in names]
        for j in range(2 * p, 2 * p + 2):
            inverse = []
            for t in range(len(names)):
                block = slice(t * SLICE, (t + 1) * SLICE)
                scores = jnp.concatenate([s_ref[j, picks[n], rows[t], :] for n in range(NSEL)], axis=1)
                scores = scores + bx_ref[batch, block, :]
                expo = jnp.exp2(scores - jnp.max(scores, axis=-1, keepdims=True))
                inverse.append(1.0 / jnp.sum(expo, axis=-1, keepdims=True))
                p_ref[batch, j, block, :] = expo.astype(BF16)
            keys = jnp.concatenate([keys_of(j, m) for m in range(NSEL // 2)], axis=0)
            summed = nn(p_ref[batch, j], keys)
            for t in range(len(names)):
                o_ref[j, rows[t], :] = summed[t * SLICE:(t + 1) * SLICE] * inverse[t]

    for name in ("B0", "B+1", "B-1"):
        for p in range(2):
            wait_bias(name, p)
    for t, name in enumerate(EARLY):
        prepare(0, t, name)
    for p in range(2):
        score("Q2", p)
        attend(0, EARLY, p)
    for name in ("A+3", "A-3", "B+3", "B-3", "B4"):
        for p in range(2):
            wait_bias(name, p)
    for t, name in enumerate(LATE):
        prepare(1, t, name)
    for p in range(2):
        attend(1, LATE, p)

    for j in range(COLS):
        mixed = o_ref[j]
        high = mixed.astype(BF16)
        low = (mixed - high.astype(F32)).astype(BF16)
        heads = nn(high, wv_ref[...]) + nn(low, wv_ref[...])
        attended = jnp.where(head == 0, heads[:TILE], 0.0)
        for h in range(1, H):
            attended = jnp.where(head == h, heads[h * TILE:(h + 1) * TILE], attended)
        rows_f32[pl.ds(j, TILE, stride=COLS), :] = gate_ref[j * TILE:(j + 1) * TILE, :] * attended
    out_ref[...] = rows_f32[...].astype(BF16)

    for _, copy in sends:
        copy.wait_send()


def on_device(
    pair,
    norm_gain,
    norm_offset,
    w_query,
    w_key,
    w_value,
    w_gate,
    gate_bias,
    w_out,
    out_bias,
    bias,
    chain_offset,
    chain_ids,
    tile_mask,
):
    hbm = pl.BlockSpec(memory_space=pltpu.HBM)
    vector = pltpu.VMEM((1, HD), F32)
    matrix = pltpu.VMEM((HD, HD), BF16)
    gated = pl.pallas_call(
        kernel,
        out_shape=jax.ShapeDtypeStruct((TILE * COLS, HD), BF16),
        in_specs=[hbm] * 12,
        out_specs=pl.BlockSpec(memory_space=pltpu.VMEM),
        scratch_shapes=[
            pltpu.VMEM((TILE * COLS, HD), BF16),
            vector,
            vector,
            matrix,
            matrix,
            matrix,
            matrix,
            vector,
            pltpu.SMEM((H,), F32),
            pltpu.VMEM((NB, TILE), jnp.int32),
            pltpu.SMEM((NB, NB), jnp.int32),
            pltpu.VMEM((NB, SLICE, TILE), BF16),
            pltpu.VMEM((NB, NSEL, SLICE, TILE), BF16),
            pltpu.VMEM((NB, 2, TILE, HD), BF16),
            pltpu.VMEM((NB, 2, TILE, HD), BF16),
            pltpu.VMEM((TILE * COLS, HD), F32),
            pltpu.VMEM((COLS, H * TILE, HD), BF16),
            pltpu.VMEM((COLS * TILE, HD), F32),
            pltpu.VMEM((TILE, TILE), jnp.int32),
            pltpu.VMEM((2, 8 * SLICE, DEPTH), F32),
            pltpu.VMEM((COLS, NB, H * TILE, TILE), F32),
            pltpu.VMEM((2, COLS, 8 * SLICE, DEPTH), BF16),
            pltpu.VMEM((COLS, H * TILE, HD), F32),
            pltpu.SemaphoreType.DMA((16,)),
            pltpu.SemaphoreType.DMA((16,)),
            pltpu.SemaphoreType.DMA((32,)),
            pltpu.SemaphoreType.DMA((30,)),
            pltpu.SemaphoreType.DMA((20,)),
            pltpu.SemaphoreType.DMA((28,)),
            pltpu.SemaphoreType.DMA((16,)),
            pltpu.SemaphoreType.DMA((16,)),
            pltpu.SemaphoreType.DMA((12,)),
        ],
        compiler_params=pltpu.CompilerParams(
            collective_id=0, has_side_effects=True, vmem_limit_bytes=64 * 1024 * 1024
        ),
        cost_estimate=pl.CostEstimate(flops=1 << 30, bytes_accessed=1 << 20, transcendentals=1 << 21),
    )(
        pair.reshape(TILE * COLS, HD),
        norm_gain.reshape(1, HD),
        norm_offset.reshape(1, HD),
        w_query,
        w_key,
        w_value,
        w_gate,
        gate_bias.reshape(1, HD),
        bias.reshape(H * TILE, TILE),
        chain_offset,
        chain_ids.reshape(NB, TILE),
        tile_mask,
    )
    update = jnp.dot(gated, w_out, preferred_element_type=F32) + out_bias
    return update.astype(BF16).reshape(TILE, COLS, HD)


def solution(mesh):
    placed = (
        P("row", "col", None),
        P(),
        P(),
        P(),
        P(),
        P(),
        P(),
        P(),
        P(),
        P(),
        P(None, "row", "col"),
        P(),
        P(),
        P(),
    )
    return jax.shard_map(
        on_device, mesh=mesh, in_specs=placed, out_specs=P("row", "col", None), check_vma=False
    )
```

```python
import functools
import math

import jax
import jax.numpy as jnp
from jax import lax
from jax.experimental import pallas as pl
from jax.experimental.pallas import tpu as pltpu
from jax.sharding import PartitionSpec as P

H = 4
DH = 32
TILE = 128
HD = 128
COLS = 4
NB = 16
NSEL = 8
SLICE = 32
DEPTH = NSEL * TILE
LOG2E = math.log2(math.e)
MESH = pl.DeviceIdType.MESH
F32 = jnp.float32
BF16 = jnp.bfloat16

BIAS_IDS = ["A+1", "A-1", "A+2", "A-2", "A+3", "A-3", "A4", "B0", "B+1", "B-1", "B+2", "B-2", "B+3", "B-3", "B4"]
NORM_IDS = ["P+1", "P-1", "P2", "Q0", "Q+1", "Q-1", "Q2"]
SIB_IDS = ["P0"] + NORM_IDS
EARLY = ["A+0", "A+1", "A-1", "B0", "B+1", "B-1", "A+2", "A-2"]
LATE = ["B+2", "B-2", "A+3", "A-3", "A4", "B+3", "B-3", "B4"]


def nt(a, b):
    return lax.dot_general(a, b, (((1,), (1,)), ((), ())), preferred_element_type=F32)


def nn(a, b):
    return jnp.dot(a, b, preferred_element_type=F32)


def kernel(
    pair_in,
    gain_in,
    shift_in,
    wq_in,
    wk_in,
    wv_in,
    wg_in,
    gb_in,
    bias_ref,
    offset_in,
    chain_in,
    mask_in,
    out_ref,
    pair_ref,
    gain_ref,
    shift_ref,
    wq_ref,
    wk_ref,
    wv_ref,
    wg_ref,
    gb_ref,
    offset_ref,
    chain_ref,
    mask_ref,
    slices_ref,
    bias_all,
    norm_0,
    norm_1,
    rows_f32,
    qp_ref,
    gate_ref,
    chain_i_ref,
    bx_ref,
    s_ref,
    p_ref,
    o_ref,
    swap_send,
    swap_recv,
    bias_send,
    bias_recv,
    norm_send,
    norm_recv,
    sib_send,
    sib_recv,
    in_sem,
):
    r = lax.axis_index("row")
    c = lax.axis_index("col")
    core, yh, x = r % 2, (r // 2) % 2, r // 4
    z, yl = c % 8, c // 8
    norm_refs = (norm_0, norm_1)

    def row_of(dx, flip):
        return ((x + dx + 4) % 4) * 4 + ((yh + flip) % 2) * 2 + core

    def col_of(dz, flip):
        return ((yl + flip) % 2) * 8 + (z + dz + 8) % 8

    up = (r, col_of(1, 0))
    down = (r, col_of(-1, 0))
    across = (r, col_of(0, 1))
    right = (row_of(1, 0), c)
    left = (row_of(-1, 0), c)
    far = (row_of(0, 1), c)
    up2 = (r, col_of(2, 0))
    down2 = (r, col_of(-2, 0))
    opposite = (row_of(2, 0), c)
    sib = (r + 1 - 2 * core, c)

    moves = [
        pltpu.make_async_copy(src, dst, in_sem.at[i])
        for i, (src, dst) in enumerate(
            (
                (pair_in, pair_ref),
                (gain_in, gain_ref),
                (shift_in, shift_ref),
                (wq_in, wq_ref),
                (wg_in, wg_ref),
                (gb_in, gb_ref),
                (wk_in, wk_ref),
                (mask_in, mask_ref),
                (offset_in, offset_ref),
                (chain_in, chain_ref),
                (wv_in, wv_ref),
                (bias_ref.at[pl.ds(c * SLICE, SLICE)], slices_ref.at[c]),
            )
        )
    ]
    for move in moves:
        move.start()

    swaps = [(flip * 8 + dz, (r, col_of(dz, flip))) for dz in (4, 3, 5, 2, 6, 1, 7, 0) for flip in (1, 0) if flip or dz]
    barrier = pltpu.get_barrier_semaphore()
    for peer in [peer for _, peer in swaps] + [right, left, far, sib, opposite]:
        pl.semaphore_signal(barrier, inc=1, device_id=peer, device_id_type=MESH)

    sends = []

    def wait_swaps():
        for index, _ in swaps:
            ref = slices_ref.at[col_of(-(index % 8), index // 8)]
            pltpu.make_async_remote_copy(
                src_ref=ref,
                dst_ref=ref,
                send_sem=swap_send.at[index],
                recv_sem=swap_recv.at[index],
                device_id=up,
                device_id_type=MESH,
            ).wait_recv()

    def bias_slot(name):
        return col_of(-int(name[1:]), 0 if name[0] == "A" else 1)

    def norm_slot(name):
        return row_of(-int(name[1:]), 0 if name[0] == "P" else 1)

    def send_bias(src_name, p, peer, as_name):
        ref = bias_all.at[bias_slot(src_name), pl.ds(p * 4, 4)]
        copy = pltpu.make_async_remote_copy(
            src_ref=ref,
            dst_ref=ref,
            send_sem=bias_send.at[len([s for s in sends if s[0] == "b"])],
            recv_sem=bias_recv.at[BIAS_IDS.index(as_name) * 2 + p],
            device_id=peer,
            device_id_type=MESH,
        )
        copy.start()
        sends.append(("b", copy))

    def wait_bias(name, p):
        ref = bias_all.at[bias_slot(name), pl.ds(p * 4, 4)]
        sem = bias_recv.at[BIAS_IDS.index(name) * 2 + p]
        pltpu.make_async_remote_copy(
            src_ref=ref, dst_ref=ref, send_sem=bias_send.at[0], recv_sem=sem, device_id=up, device_id_type=MESH
        ).wait_recv()

    def norm_part(name, p, e):
        ref = norm_refs[p].at[norm_slot(name)]
        return ref if e is None else ref.at[e]

    def norm_sem(name, p, e):
        return norm_recv.at[(NORM_IDS.index(name) * 2 + p) * 2 + (0 if e is None else e)]

    def send_norm(src_name, p, e, peer, as_name):
        ref = norm_part(src_name, p, e)
        copy = pltpu.make_async_remote_copy(
            src_ref=ref,
            dst_ref=ref,
            send_sem=norm_send.at[len([s for s in sends if s[0] == "n"])],
            recv_sem=norm_sem(as_name, p, e),
            device_id=peer,
            device_id_type=MESH,
        )
        copy.start()
        sends.append(("n", copy))

    def wait_norm(name, p, e=None):
        ref = norm_part(name, p, e)
        pltpu.make_async_remote_copy(
            src_ref=ref,
            dst_ref=ref,
            send_sem=norm_send.at[0],
            recv_sem=norm_sem(name, p, e),
            device_id=up,
            device_id_type=MESH,
        ).wait_recv()

    def send_sib(name, p):
        ref = norm_refs[p].at[norm_slot(name)]
        index = SIB_IDS.index(name) * 2 + p
        copy = pltpu.make_async_remote_copy(
            src_ref=ref,
            dst_ref=ref,
            send_sem=sib_send.at[index],
            recv_sem=sib_recv.at[index],
            device_id=sib,
            device_id_type=MESH,
        )
        copy.start()
        sends.append(("s", copy))

    def wait_sib(name, p):
        ref = norm_refs[p].at[norm_slot(name) + 1 - 2 * core]
        index = SIB_IDS.index(name) * 2 + p
        pltpu.make_async_remote_copy(
            src_ref=ref,
            dst_ref=ref,
            send_sem=sib_send.at[index],
            recv_sem=sib_recv.at[index],
            device_id=sib,
            device_id_type=MESH,
        ).wait_recv()

    for move in moves[:3]:
        move.wait()
    values = pair_ref[...].astype(F32)
    center = values - jnp.mean(values, -1, keepdims=True)
    spread = jnp.mean(center * center, -1, keepdims=True)
    rows_f32[...] = center * lax.rsqrt(spread + 1e-05) * gain_ref[...] + shift_ref[...]
    for p in range(2):
        for e in range(2):
            norm_refs[p][r, e] = rows_f32[pl.ds(2 * p + e, TILE, stride=COLS), :].astype(BF16)

    pl.semaphore_wait(barrier, 20)
    for p in range(2):
        send_norm("P0", p, None, far, "Q0")
        send_norm("P0", p, None, right, "P+1")
        send_norm("P0", p, None, left, "P-1")

    for index, peer in swaps:
        copy = pltpu.make_async_remote_copy(
            src_ref=bias_ref.at[pl.ds(peer[1] * SLICE, SLICE)],
            dst_ref=slices_ref.at[c],
            send_sem=swap_send.at[index],
            recv_sem=swap_recv.at[index],
            device_id=peer,
            device_id_type=MESH,
        )
        copy.start()
        sends.append(("w", copy))

    for p in range(2):
        send_sib("P0", p)
    for move in moves[3:]:
        move.wait()

    picks = [jnp.int32(0) for _ in range(NSEL)]
    count = jnp.int32(0)
    for k in range(NB):
        flag = mask_ref[r, k]
        for n in range(NSEL):
            picks[n] = jnp.where((flag == 1) & (count == n), k, picks[n])
        count = count + jnp.where(flag == 1, 1, 0)
    pads = [jnp.where(n < count, 0.0, -1e30).astype(F32) for n in range(NSEL)]

    mine = jnp.concatenate([norm_refs[p][r].reshape(2 * TILE, HD) for p in range(2)], axis=0)
    query = (nn(mine, wq_ref[...]) * (1.0 / DH**0.5)).astype(BF16)
    head = lax.broadcasted_iota(jnp.int32, (TILE, HD), 1) // DH
    for j in range(COLS):
        part = query[j * TILE:(j + 1) * TILE]
        stacked = jnp.concatenate([jnp.where(head == h, part, jnp.zeros_like(part)) for h in range(H)], axis=0)
        qp_ref[j] = (nt(stacked, wk_ref[...]) * LOG2E).astype(BF16)

    gate_ref[...] = jax.nn.sigmoid(nn(mine, wg_ref[...]) + gb_ref[...])
    chain_i_ref[...] = jnp.transpose(jnp.broadcast_to(chain_ref[pl.ds(r, 1), :], (TILE, TILE)))

    def keys_of(j, m):
        return jnp.concatenate([norm_refs[j // 2][picks[2 * m + e], j % 2] for e in range(2)], axis=0)

    def score(name, p):
        wait_sib(name, p)
        first = norm_slot(name) - core
        for e in range(2):
            keys = norm_refs[p][pl.ds(first, 2), e].reshape(2 * TILE, HD)
            both = nt(qp_ref[2 * p + e], keys)
            s_ref[2 * p + e, first] = both[:, :TILE]
            s_ref[2 * p + e, first + 1] = both[:, TILE:]

    def pass_first(p):
        wait_norm("Q0", p)
        send_norm("Q0", p, None, opposite, "Q2")
        send_norm("Q0", p, None, right, "Q+1")
        send_norm("Q0", p, None, left, "Q-1")
        wait_norm("P+1", p)
        send_norm("P+1", p, 0, right, "P2")
        wait_norm("P-1", p)
        send_norm("P-1", p, 1, left, "P2")
        for name in ("P+1", "P-1", "Q0"):
            send_sib(name, p)

    def pass_second(p):
        wait_norm("P2", p, 0)
        wait_norm("P2", p, 1)
        for name in ("Q+1", "Q-1"):
            wait_norm(name, p)
        for name in ("P2", "Q+1", "Q-1"):
            send_sib(name, p)

    for p in range(2):
        score("P0", p)
    pass_first(0)
    wait_swaps()
    for n in range(NSEL):
        bias_all[c, n] = slices_ref[picks[n]]
    for p in range(2):
        send_bias("A0", p, up, "A+1")
        send_bias("A0", p, down, "A-1")
        send_bias("A0", p, across, "B0")
    for p in range(2):
        send_bias("A0", p, up2, "A+2")
        send_bias("A0", p, down2, "A-2")
    pass_first(1)
    for name in ("P+1", "P-1", "Q0"):
        score(name, 0)
    for p in range(2):
        wait_bias("B0", p)
        send_bias("B0", p, up, "B+1")
        send_bias("B0", p, down, "B-1")
    for name in ("P+1", "P-1", "Q0"):
        score(name, 1)
    for p in range(2):
        wait_bias("A+2", p)
        if p == 0:
            send_bias("A+2", p, up2, "A4")
        send_bias("A+2", p, across, "B+2")
        send_bias("A+2", p, up, "A+3")
        wait_bias("A-2", p)
        if p == 1:
            send_bias("A-2", p, down2, "A4")
        send_bias("A-2", p, across, "B-2")
        send_bias("A-2", p, down, "A-3")
    pass_second(0)
    wait_norm("Q2", 0)
    send_sib("Q2", 0)
    for name in ("P2", "Q+1", "Q-1"):
        score(name, 0)
    pass_second(1)
    for p in range(2):
        wait_bias("B+2", p)
        send_bias("B+2", p, up, "B+3")
        wait_bias("B-2", p)
        send_bias("B-2", p, down, "B-3")
        wait_bias("A4", p)
        send_bias("A4", p, across, "B4")
    wait_norm("Q2", 1)
    send_sib("Q2", 1)
    score("Q2", 0)

    def prepare(batch, t, name):
        slot = bias_slot(name)
        chain_i = chain_i_ref[pl.ds(pl.multiple_of((slot % 4) * SLICE, SLICE), SLICE), :]
        extra = offset_ref[slot // 4]
        for n in range(NSEL):
            differs = chain_i != chain_ref[pl.ds(picks[n], 1), :]
            part = (bias_all[slot, n].astype(F32) + jnp.where(differs, extra, 0.0) + pads[n]) * LOG2E
            bx_ref[batch, t * SLICE:(t + 1) * SLICE, n * TILE:(n + 1) * TILE] = part

    def attend(batch, names, p):
        rows = [pl.ds(pl.multiple_of(bias_slot(name) * SLICE, SLICE), SLICE) for name in names]
        for j in range(2 * p, 2 * p + 2):
            inverse = []
            for t in range(len(names)):
                block = slice(t * SLICE, (t + 1) * SLICE)
                scores = jnp.concatenate([s_ref[j, picks[n], rows[t], :] for n in range(NSEL)], axis=1)
                scores = scores + bx_ref[batch, block, :]
                expo = jnp.exp2(scores - jnp.max(scores, axis=-1, keepdims=True))
                inverse.append(1.0 / jnp.sum(expo, axis=-1, keepdims=True))
                p_ref[batch, j, block, :] = expo.astype(BF16)
            keys = jnp.concatenate([keys_of(j, m) for m in range(NSEL // 2)], axis=0)
            summed = nn(p_ref[batch, j], keys)
            for t in range(len(names)):
                o_ref[j, rows[t], :] = summed[t * SLICE:(t + 1) * SLICE] * inverse[t]

    for name in ("A+1", "A-1", "B+1", "B-1"):
        for p in range(2):
            wait_bias(name, p)
    for t, name in enumerate(EARLY):
        prepare(0, t, name)
    attend(0, EARLY, 0)
    for name in ("P2", "Q+1", "Q-1", "Q2"):
        score(name, 1)
    attend(0, EARLY, 1)
    for name in ("A+3", "A-3", "B+3", "B-3", "B4"):
        for p in range(2):
            wait_bias(name, p)
    for t, name in enumerate(LATE):
        prepare(1, t, name)
    for p in range(2):
        attend(1, LATE, p)

    for j in range(COLS):
        mixed = o_ref[j]
        high = mixed.astype(BF16)
        low = (mixed - high.astype(F32)).astype(BF16)
        heads = nn(high, wv_ref[...]) + nn(low, wv_ref[...])
        attended = jnp.where(head == 0, heads[:TILE], 0.0)
        for h in range(1, H):
            attended = jnp.where(head == h, heads[h * TILE:(h + 1) * TILE], attended)
        rows_f32[pl.ds(j, TILE, stride=COLS), :] = gate_ref[j * TILE:(j + 1) * TILE, :] * attended
    out_ref[...] = rows_f32[...].astype(BF16)

    for _, copy in sends:
        copy.wait_send()


def on_device(
    pair,
    norm_gain,
    norm_offset,
    w_query,
    w_key,
    w_value,
    w_gate,
    gate_bias,
    w_out,
    out_bias,
    bias,
    chain_offset,
    chain_ids,
    tile_mask,
):
    hbm = pl.BlockSpec(memory_space=pltpu.HBM)
    vector = pltpu.VMEM((1, HD), F32)
    matrix = pltpu.VMEM((HD, HD), BF16)
    gated = pl.pallas_call(
        kernel,
        out_shape=jax.ShapeDtypeStruct((TILE * COLS, HD), BF16),
        in_specs=[hbm] * 12,
        out_specs=pl.BlockSpec(memory_space=pltpu.VMEM),
        scratch_shapes=[
            pltpu.VMEM((TILE * COLS, HD), BF16),
            vector,
            vector,
            matrix,
            matrix,
            matrix,
            matrix,
            vector,
            pltpu.SMEM((H,), F32),
            pltpu.VMEM((NB, TILE), jnp.int32),
            pltpu.SMEM((NB, NB), jnp.int32),
            pltpu.VMEM((NB, SLICE, TILE), BF16),
            pltpu.VMEM((NB, NSEL, SLICE, TILE), BF16),
            pltpu.VMEM((NB, 2, TILE, HD), BF16),
            pltpu.VMEM((NB, 2, TILE, HD), BF16),
            pltpu.VMEM((TILE * COLS, HD), F32),
            pltpu.VMEM((COLS, H * TILE, HD), BF16),
            pltpu.VMEM((COLS * TILE, HD), F32),
            pltpu.VMEM((TILE, TILE), jnp.int32),
            pltpu.VMEM((2, 8 * SLICE, DEPTH), F32),
            pltpu.VMEM((COLS, NB, H * TILE, TILE), F32),
            pltpu.VMEM((2, COLS, 8 * SLICE, DEPTH), BF16),
            pltpu.VMEM((COLS, H * TILE, HD), F32),
            pltpu.SemaphoreType.DMA((16,)),
            pltpu.SemaphoreType.DMA((16,)),
            pltpu.SemaphoreType.DMA((32,)),
            pltpu.SemaphoreType.DMA((30,)),
            pltpu.SemaphoreType.DMA((20,)),
            pltpu.SemaphoreType.DMA((28,)),
            pltpu.SemaphoreType.DMA((16,)),
            pltpu.SemaphoreType.DMA((16,)),
            pltpu.SemaphoreType.DMA((12,)),
        ],
        compiler_params=pltpu.CompilerParams(
            collective_id=0, has_side_effects=True, vmem_limit_bytes=64 * 1024 * 1024
        ),
        cost_estimate=pl.CostEstimate(flops=1 << 30, bytes_accessed=1 << 20, transcendentals=1 << 21),
    )(
        pair.reshape(TILE * COLS, HD),
        norm_gain.reshape(1, HD),
        norm_offset.reshape(1, HD),
        w_query,
        w_key,
        w_value,
        w_gate,
        gate_bias.reshape(1, HD),
        bias.reshape(H * TILE, TILE),
        chain_offset,
        chain_ids.reshape(NB, TILE),
        tile_mask,
    )
    update = jnp.dot(gated, w_out, preferred_element_type=F32) + out_bias
    return update.astype(BF16).reshape(TILE, COLS, HD)


def solution(mesh):
    placed = (
        P("row", "col", None),
        P(),
        P(),
        P(),
        P(),
        P(),
        P(),
        P(),
        P(),
        P(),
        P(None, "row", "col"),
        P(),
        P(),
        P(),
    )
    return jax.shard_map(
        on_device, mesh=mesh, in_specs=placed, out_specs=P("row", "col", None), check_vma=False
    )
```

```python
import functools
import math

import jax
import jax.numpy as jnp
from jax import lax
from jax.experimental import pallas as pl
from jax.experimental.pallas import tpu as pltpu
from jax.sharding import PartitionSpec as P

H = 4
DH = 32
TILE = 128
HD = 128
COLS = 4
NB = 16
NSEL = 8
SLICE = 32
DEPTH = NSEL * TILE
LOG2E = math.log2(math.e)
MESH = pl.DeviceIdType.MESH
F32 = jnp.float32
BF16 = jnp.bfloat16

BIAS_IDS = ["A+1", "A-1", "A+2", "A-2", "A+3", "A-3", "A4", "B0", "B+1", "B-1", "B+2", "B-2", "B+3", "B-3", "B4"]
NORM_IDS = ["P+1", "P-1", "P2", "Q0", "Q+1", "Q-1", "Q2"]
SIB_IDS = ["P0"] + NORM_IDS
EARLY = ["A+0", "A+1", "A-1", "B0", "B+1", "B-1", "A+2", "A-2"]
LATE = ["B+2", "B-2", "A+3", "A-3", "A4", "B+3", "B-3", "B4"]


def nt(a, b):
    return lax.dot_general(a, b, (((1,), (1,)), ((), ())), preferred_element_type=F32)


def nn(a, b):
    return jnp.dot(a, b, preferred_element_type=F32)


def kernel(
    pair_in,
    gain_in,
    shift_in,
    wq_in,
    wk_in,
    wv_in,
    wg_in,
    gb_in,
    bias_ref,
    offset_in,
    chain_in,
    mask_in,
    out_ref,
    pair_ref,
    gain_ref,
    shift_ref,
    wq_ref,
    wk_ref,
    wv_ref,
    wg_ref,
    gb_ref,
    offset_ref,
    chain_ref,
    mask_ref,
    slices_ref,
    bias_all,
    norm_0,
    norm_1,
    rows_f32,
    qp_ref,
    gate_ref,
    chain_i_ref,
    bx_ref,
    s_ref,
    p_ref,
    o_ref,
    swap_send,
    swap_recv,
    bias_send,
    bias_recv,
    norm_send,
    norm_recv,
    sib_send,
    sib_recv,
    in_sem,
):
    r = lax.axis_index("row")
    c = lax.axis_index("col")
    core, yh, x = r % 2, (r // 2) % 2, r // 4
    z, yl = c % 8, c // 8
    norm_refs = (norm_0, norm_1)

    def row_of(dx, flip):
        return ((x + dx + 4) % 4) * 4 + ((yh + flip) % 2) * 2 + core

    def col_of(dz, flip):
        return ((yl + flip) % 2) * 8 + (z + dz + 8) % 8

    up = (r, col_of(1, 0))
    down = (r, col_of(-1, 0))
    across = (r, col_of(0, 1))
    right = (row_of(1, 0), c)
    left = (row_of(-1, 0), c)
    far = (row_of(0, 1), c)
    up2 = (r, col_of(2, 0))
    down2 = (r, col_of(-2, 0))
    opposite = (row_of(2, 0), c)
    sib = (r + 1 - 2 * core, c)

    moves = [
        pltpu.make_async_copy(src, dst, in_sem.at[i])
        for i, (src, dst) in enumerate(
            (
                (pair_in, pair_ref),
                (gain_in, gain_ref),
                (shift_in, shift_ref),
                (wq_in, wq_ref),
                (wg_in, wg_ref),
                (gb_in, gb_ref),
                (wk_in, wk_ref),
                (mask_in, mask_ref),
                (offset_in, offset_ref),
                (chain_in, chain_ref),
                (wv_in, wv_ref),
                (bias_ref.at[pl.ds(c * SLICE, SLICE)], slices_ref.at[c]),
            )
        )
    ]
    for move in moves:
        move.start()

    swaps = [(flip * 8 + dz, (r, col_of(dz, flip))) for dz in (4, 3, 5, 2, 6, 1, 7, 0) for flip in (1, 0) if flip or dz]
    barrier = pltpu.get_barrier_semaphore()
    for peer in [peer for _, peer in swaps] + [right, left, far, sib, opposite]:
        pl.semaphore_signal(barrier, inc=1, device_id=peer, device_id_type=MESH)

    sends = []

    def wait_swaps():
        for index, _ in swaps:
            ref = slices_ref.at[col_of(-(index % 8), index // 8)]
            pltpu.make_async_remote_copy(
                src_ref=ref,
                dst_ref=ref,
                send_sem=swap_send.at[index],
                recv_sem=swap_recv.at[index],
                device_id=up,
                device_id_type=MESH,
            ).wait_recv()

    def bias_slot(name):
        return col_of(-int(name[1:]), 0 if name[0] == "A" else 1)

    def norm_slot(name):
        return row_of(-int(name[1:]), 0 if name[0] == "P" else 1)

    def send_bias(src_name, p, peer, as_name):
        ref = bias_all.at[bias_slot(src_name), pl.ds(p * 4, 4)]
        copy = pltpu.make_async_remote_copy(
            src_ref=ref,
            dst_ref=ref,
            send_sem=bias_send.at[len([s for s in sends if s[0] == "b"])],
            recv_sem=bias_recv.at[BIAS_IDS.index(as_name) * 2 + p],
            device_id=peer,
            device_id_type=MESH,
        )
        copy.start()
        sends.append(("b", copy))

    def wait_bias(name, p):
        ref = bias_all.at[bias_slot(name), pl.ds(p * 4, 4)]
        sem = bias_recv.at[BIAS_IDS.index(name) * 2 + p]
        pltpu.make_async_remote_copy(
            src_ref=ref, dst_ref=ref, send_sem=bias_send.at[0], recv_sem=sem, device_id=up, device_id_type=MESH
        ).wait_recv()

    def norm_part(name, p, e):
        ref = norm_refs[p].at[norm_slot(name)]
        return ref if e is None else ref.at[e]

    def norm_sem(name, p, e):
        return norm_recv.at[(NORM_IDS.index(name) * 2 + p) * 2 + (0 if e is None else e)]

    def send_norm(src_name, p, e, peer, as_name):
        ref = norm_part(src_name, p, e)
        copy = pltpu.make_async_remote_copy(
            src_ref=ref,
            dst_ref=ref,
            send_sem=norm_send.at[len([s for s in sends if s[0] == "n"])],
            recv_sem=norm_sem(as_name, p, e),
            device_id=peer,
            device_id_type=MESH,
        )
        copy.start()
        sends.append(("n", copy))

    def wait_norm(name, p, e=None):
        ref = norm_part(name, p, e)
        pltpu.make_async_remote_copy(
            src_ref=ref,
            dst_ref=ref,
            send_sem=norm_send.at[0],
            recv_sem=norm_sem(name, p, e),
            device_id=up,
            device_id_type=MESH,
        ).wait_recv()

    def send_sib(name, p):
        ref = norm_refs[p].at[norm_slot(name)]
        index = SIB_IDS.index(name) * 2 + p
        copy = pltpu.make_async_remote_copy(
            src_ref=ref,
            dst_ref=ref,
            send_sem=sib_send.at[index],
            recv_sem=sib_recv.at[index],
            device_id=sib,
            device_id_type=MESH,
        )
        copy.start()
        sends.append(("s", copy))

    def wait_sib(name, p):
        ref = norm_refs[p].at[norm_slot(name) + 1 - 2 * core]
        index = SIB_IDS.index(name) * 2 + p
        pltpu.make_async_remote_copy(
            src_ref=ref,
            dst_ref=ref,
            send_sem=sib_send.at[index],
            recv_sem=sib_recv.at[index],
            device_id=sib,
            device_id_type=MESH,
        ).wait_recv()

    for move in moves[:3]:
        move.wait()
    values = pair_ref[...].astype(F32)
    center = values - jnp.mean(values, -1, keepdims=True)
    spread = jnp.mean(center * center, -1, keepdims=True)
    rows_f32[...] = center * lax.rsqrt(spread + 1e-05) * gain_ref[...] + shift_ref[...]
    for p in range(2):
        for e in range(2):
            norm_refs[p][r, e] = rows_f32[pl.ds(2 * p + e, TILE, stride=COLS), :].astype(BF16)

    pl.semaphore_wait(barrier, 20)
    for p in range(2):
        send_norm("P0", p, None, far, "Q0")
        send_norm("P0", p, None, right, "P+1")
        send_norm("P0", p, None, left, "P-1")

    for index, peer in swaps:
        copy = pltpu.make_async_remote_copy(
            src_ref=bias_ref.at[pl.ds(peer[1] * SLICE, SLICE)],
            dst_ref=slices_ref.at[c],
            send_sem=swap_send.at[index],
            recv_sem=swap_recv.at[index],
            device_id=peer,
            device_id_type=MESH,
        )
        copy.start()
        sends.append(("w", copy))

    for p in range(2):
        send_sib("P0", p)
    for move in moves[3:]:
        move.wait()

    picks = [jnp.int32(0) for _ in range(NSEL)]
    count = jnp.int32(0)
    for k in range(NB):
        flag = mask_ref[r, k]
        for n in range(NSEL):
            picks[n] = jnp.where((flag == 1) & (count == n), k, picks[n])
        count = count + jnp.where(flag == 1, 1, 0)
    pads = [jnp.where(n < count, 0.0, -1e30).astype(F32) for n in range(NSEL)]

    def keys_of(j, m):
        return jnp.concatenate([norm_refs[j // 2][picks[2 * m + e], j % 2] for e in range(2)], axis=0)

    def score(name, p):
        wait_sib(name, p)
        first = norm_slot(name) - core
        for e in range(2):
            keys = norm_refs[p][pl.ds(first, 2), e].reshape(2 * TILE, HD)
            both = nt(qp_ref[2 * p + e], keys)
            s_ref[2 * p + e, first] = both[:, :TILE]
            s_ref[2 * p + e, first + 1] = both[:, TILE:]

    def pass_first(p):
        wait_norm("Q0", p)
        send_norm("Q0", p, None, opposite, "Q2")
        send_norm("Q0", p, None, right, "Q+1")
        send_norm("Q0", p, None, left, "Q-1")
        wait_norm("P+1", p)
        send_norm("P+1", p, 0, right, "P2")
        wait_norm("P-1", p)
        send_norm("P-1", p, 1, left, "P2")
        for name in ("P+1", "P-1", "Q0"):
            send_sib(name, p)

    def pass_second(p):
        wait_norm("P2", p, 0)
        wait_norm("P2", p, 1)
        for name in ("Q+1", "Q-1"):
            wait_norm(name, p)
        for name in ("P2", "Q+1", "Q-1"):
            send_sib(name, p)

    pass_first(0)
    wait_swaps()
    for n in range(NSEL):
        bias_all[c, n] = slices_ref[picks[n]]
    for p in range(2):
        send_bias("A0", p, up, "A+1")
        send_bias("A0", p, down, "A-1")
        send_bias("A0", p, across, "B0")
    for p in range(2):
        send_bias("A0", p, up2, "A+2")
        send_bias("A0", p, down2, "A-2")
    mine = jnp.concatenate([norm_refs[p][r].reshape(2 * TILE, HD) for p in range(2)], axis=0)
    query = (nn(mine, wq_ref[...]) * (1.0 / DH**0.5)).astype(BF16)
    head = lax.broadcasted_iota(jnp.int32, (TILE, HD), 1) // DH
    for j in range(COLS):
        part = query[j * TILE:(j + 1) * TILE]
        stacked = jnp.concatenate([jnp.where(head == h, part, jnp.zeros_like(part)) for h in range(H)], axis=0)
        qp_ref[j] = (nt(stacked, wk_ref[...]) * LOG2E).astype(BF16)

    gate_ref[...] = jax.nn.sigmoid(nn(mine, wg_ref[...]) + gb_ref[...])
    chain_i_ref[...] = jnp.transpose(jnp.broadcast_to(chain_ref[pl.ds(r, 1), :], (TILE, TILE)))

    pass_first(1)
    for p in range(2):
        score("P0", p)
    for name in ("P+1", "P-1", "Q0"):
        score(name, 0)
    for p in range(2):
        wait_bias("B0", p)
        send_bias("B0", p, up, "B+1")
        send_bias("B0", p, down, "B-1")
    for name in ("P+1", "P-1", "Q0"):
        score(name, 1)
    for p in range(2):
        wait_bias("A+2", p)
        if p == 0:
            send_bias("A+2", p, up2, "A4")
        send_bias("A+2", p, across, "B+2")
        send_bias("A+2", p, up, "A+3")
        wait_bias("A-2", p)
        if p == 1:
            send_bias("A-2", p, down2, "A4")
        send_bias("A-2", p, across, "B-2")
        send_bias("A-2", p, down, "A-3")
    pass_second(0)
    wait_norm("Q2", 0)
    send_sib("Q2", 0)
    for name in ("P2", "Q+1", "Q-1"):
        score(name, 0)
    pass_second(1)
    for p in range(2):
        wait_bias("B+2", p)
        send_bias("B+2", p, up, "B+3")
        wait_bias("B-2", p)
        send_bias("B-2", p, down, "B-3")
        wait_bias("A4", p)
        send_bias("A4", p, across, "B4")
    wait_norm("Q2", 1)
    send_sib("Q2", 1)
    score("Q2", 0)

    def prepare(batch, t, name):
        slot = bias_slot(name)
        chain_i = chain_i_ref[pl.ds(pl.multiple_of((slot % 4) * SLICE, SLICE), SLICE), :]
        extra = offset_ref[slot // 4]
        for n in range(NSEL):
            differs = chain_i != chain_ref[pl.ds(picks[n], 1), :]
            part = (bias_all[slot, n].astype(F32) + jnp.where(differs, extra, 0.0) + pads[n]) * LOG2E
            bx_ref[batch, t * SLICE:(t + 1) * SLICE, n * TILE:(n + 1) * TILE] = part

    def attend(batch, names, p):
        rows = [pl.ds(pl.multiple_of(bias_slot(name) * SLICE, SLICE), SLICE) for name in names]
        for j in range(2 * p, 2 * p + 2):
            inverse = []
            for t in range(len(names)):
                block = slice(t * SLICE, (t + 1) * SLICE)
                scores = jnp.concatenate([s_ref[j, picks[n], rows[t], :] for n in range(NSEL)], axis=1)
                scores = scores + bx_ref[batch, block, :]
                expo = jnp.exp2(scores - jnp.max(scores, axis=-1, keepdims=True))
                inverse.append(1.0 / jnp.sum(expo, axis=-1, keepdims=True))
                p_ref[batch, j, block, :] = expo.astype(BF16)
            keys = jnp.concatenate([keys_of(j, m) for m in range(NSEL // 2)], axis=0)
            summed = nn(p_ref[batch, j], keys)
            for t in range(len(names)):
                o_ref[j, rows[t], :] = summed[t * SLICE:(t + 1) * SLICE] * inverse[t]

    for name in ("A+1", "A-1", "B+1", "B-1"):
        for p in range(2):
            wait_bias(name, p)
    for t, name in enumerate(EARLY):
        prepare(0, t, name)
    attend(0, EARLY, 0)
    for name in ("P2", "Q+1", "Q-1", "Q2"):
        score(name, 1)
    attend(0, EARLY, 1)
    for name in ("A+3", "A-3", "B+3", "B-3", "B4"):
        for p in range(2):
            wait_bias(name, p)
    for t, name in enumerate(LATE):
        prepare(1, t, name)
    for p in range(2):
        attend(1, LATE, p)

    for j in range(COLS):
        mixed = o_ref[j]
        high = mixed.astype(BF16)
        low = (mixed - high.astype(F32)).astype(BF16)
        heads = nn(high, wv_ref[...]) + nn(low, wv_ref[...])
        attended = jnp.where(head == 0, heads[:TILE], 0.0)
        for h in range(1, H):
            attended = jnp.where(head == h, heads[h * TILE:(h + 1) * TILE], attended)
        rows_f32[pl.ds(j, TILE, stride=COLS), :] = gate_ref[j * TILE:(j + 1) * TILE, :] * attended
    out_ref[...] = rows_f32[...].astype(BF16)

    for _, copy in sends:
        copy.wait_send()


def on_device(
    pair,
    norm_gain,
    norm_offset,
    w_query,
    w_key,
    w_value,
    w_gate,
    gate_bias,
    w_out,
    out_bias,
    bias,
    chain_offset,
    chain_ids,
    tile_mask,
):
    hbm = pl.BlockSpec(memory_space=pltpu.HBM)
    vector = pltpu.VMEM((1, HD), F32)
    matrix = pltpu.VMEM((HD, HD), BF16)
    gated = pl.pallas_call(
        kernel,
        out_shape=jax.ShapeDtypeStruct((TILE * COLS, HD), BF16),
        in_specs=[hbm] * 12,
        out_specs=pl.BlockSpec(memory_space=pltpu.VMEM),
        scratch_shapes=[
            pltpu.VMEM((TILE * COLS, HD), BF16),
            vector,
            vector,
            matrix,
            matrix,
            matrix,
            matrix,
            vector,
            pltpu.SMEM((H,), F32),
            pltpu.VMEM((NB, TILE), jnp.int32),
            pltpu.SMEM((NB, NB), jnp.int32),
            pltpu.VMEM((NB, SLICE, TILE), BF16),
            pltpu.VMEM((NB, NSEL, SLICE, TILE), BF16),
            pltpu.VMEM((NB, 2, TILE, HD), BF16),
            pltpu.VMEM((NB, 2, TILE, HD), BF16),
            pltpu.VMEM((TILE * COLS, HD), F32),
            pltpu.VMEM((COLS, H * TILE, HD), BF16),
            pltpu.VMEM((COLS * TILE, HD), F32),
            pltpu.VMEM((TILE, TILE), jnp.int32),
            pltpu.VMEM((2, 8 * SLICE, DEPTH), F32),
            pltpu.VMEM((COLS, NB, H * TILE, TILE), F32),
            pltpu.VMEM((2, COLS, 8 * SLICE, DEPTH), BF16),
            pltpu.VMEM((COLS, H * TILE, HD), F32),
            pltpu.SemaphoreType.DMA((16,)),
            pltpu.SemaphoreType.DMA((16,)),
            pltpu.SemaphoreType.DMA((32,)),
            pltpu.SemaphoreType.DMA((30,)),
            pltpu.SemaphoreType.DMA((20,)),
            pltpu.SemaphoreType.DMA((28,)),
            pltpu.SemaphoreType.DMA((16,)),
            pltpu.SemaphoreType.DMA((16,)),
            pltpu.SemaphoreType.DMA((12,)),
        ],
        compiler_params=pltpu.CompilerParams(
            collective_id=0, has_side_effects=True, vmem_limit_bytes=64 * 1024 * 1024
        ),
        cost_estimate=pl.CostEstimate(flops=1 << 30, bytes_accessed=1 << 20, transcendentals=1 << 21),
    )(
        pair.reshape(TILE * COLS, HD),
        norm_gain.reshape(1, HD),
        norm_offset.reshape(1, HD),
        w_query,
        w_key,
        w_value,
        w_gate,
        gate_bias.reshape(1, HD),
        bias.reshape(H * TILE, TILE),
        chain_offset,
        chain_ids.reshape(NB, TILE),
        tile_mask,
    )
    update = jnp.dot(gated, w_out, preferred_element_type=F32) + out_bias
    return update.astype(BF16).reshape(TILE, COLS, HD)


def solution(mesh):
    placed = (
        P("row", "col", None),
        P(),
        P(),
        P(),
        P(),
        P(),
        P(),
        P(),
        P(),
        P(),
        P(None, "row", "col"),
        P(),
        P(),
        P(),
    )
    return jax.shard_map(
        on_device, mesh=mesh, in_specs=placed, out_specs=P("row", "col", None), check_vma=False
    )
```
